128 devices in a mesh: dp: 4 (over y), seq: 32 (over x, z, core).
Axes of the slice: x: 4, y: 4, z: 4, core: 2. Of those that a mesh axis runs over, the one named last changes fastest.
Arguments:
- queries: bfloat16 [4, 4096, 1024], P('dp', 'seq'), may hold values from -6 to 6
- keys: bfloat16 [4, 4096, 1024], P('dp', 'seq'), may hold values from -6 to 6
- values: bfloat16 [4, 4096, 1024], P('dp', 'seq'), may hold values from -6 to 6
- strength: bfloat16 [4, 4096, 8], P('dp', 'seq'), may hold values from 0 to 1
- log_decay: float32 [4, 4096, 8], P('dp', 'seq'), may hold values from -2 to 0
- resets: int32 [4, 64], P('dp', 'seq'), may hold values 0 or 1
- out_weight: bfloat16 [1024, 2048], replicated, may hold values from -0.1875 to 0.1875
- cotangent: bfloat16 [4, 4096, 2048], P('dp', 'seq'), may hold values from -6 to 6
Outputs:
- mixed: bfloat16 [4, 4096, 2048], P('dp', 'seq')
- query_grad: bfloat16 [4, 4096, 1024], P('dp', 'seq')
- key_grad: bfloat16 [4, 4096, 1024], P('dp', 'seq')
- value_grad: bfloat16 [4, 4096, 1024], P('dp', 'seq')
- strength_grad: float32 [4, 4096, 8], P('dp', 'seq')
- decay_grad: float32 [4, 4096, 8], P('dp', 'seq')
- weight_grad: float32 [1024, 2048], P(('dp', 'seq'))
The draws below stay inside these ranges and needn't reach their ends.
All inputs are finite; a program needn't handle non-finite values. No bound on the sum of `resets` on one device may be relied on, other than what follows from the above.
Results may differ from the reference program's by a relative error of at most 0.0049.
Values sent between devices are 32-bit elements; how exact they have to be, the bound alone decides.
No kernel may reach another device: no remote copies, remote signals or barrier semaphores. Data moves between devices by JAX's collectives and lax.ppermute only.
A program may use at most 192 MiB of HBM per device.

```python
import math
import jax
import jax.numpy as jnp
from jax import lax

D = 2048
H = 8
DK = 128
SPAN = 64
TOK_DEV = 128
HK = 1024
SEQUENCE_GROUPS = 4
SEQUENCE_LENGTH = 4096
SPANS = 64
N_SEQ = 32


def head_kinds(key, share):
    return jax.random.uniform(jax.random.fold_in(key, 101), (SEQUENCE_GROUPS, 1, H)) < share


def draw_log_decay(key, part):
    share = 0.5
    rough_lo, rough_hi = (0.5, 1.5)
    fast = head_kinds(key, share)
    key = jax.random.fold_in(key, 7)
    key_collection = jax.random.split(key, 6)
    slow_rate = jax.random.uniform(key_collection[0], (SEQUENCE_GROUPS, 1, H), minval=0.1, maxval=0.4) / SEQUENCE_LENGTH
    fast_rate = jax.random.uniform(key_collection[1], (SEQUENCE_GROUPS, 1, H), minval=1.0 / 50.0, maxval=1.0 / 30.0)
    learning_rate = jnp.where(fast, fast_rate, slow_rate)
    blocks = SEQUENCE_LENGTH // TOK_DEV
    multiplier = jnp.exp(jax.random.uniform(key_collection[2], (SEQUENCE_GROUPS, blocks, 1, H), minval=-0.7, maxval=0.7))
    multiplier = jnp.broadcast_to(multiplier, (SEQUENCE_GROUPS, blocks, TOK_DEV, H)).reshape(SEQUENCE_GROUPS, SEQUENCE_LENGTH, H)
    coarse_estimate = jax.random.uniform(key_collection[3], (SEQUENCE_GROUPS, SEQUENCE_LENGTH, H), minval=rough_lo, maxval=rough_hi)
    sudden_spike = jax.random.uniform(key_collection[4], (SEQUENCE_GROUPS, SEQUENCE_LENGTH, 1)) < 2.0 / SEQUENCE_LENGTH
    training_loss = jnp.log(jax.random.uniform(key_collection[5], (SEQUENCE_GROUPS, SEQUENCE_LENGTH, 1), minval=0.5, maxval=0.8))
    decay_factor = -(learning_rate * multiplier * coarse_estimate) + jnp.where(sudden_spike, training_loss, 0.0)
    return decay_factor.astype(jnp.float32)


def draw_strength(key, part):
    share = 0.5
    rough_lo, rough_hi = (0.5, 1.5)
    strong_lo, strong_hi = (0.2, 0.9)
    fast = head_kinds(key, share)
    key = jax.random.fold_in(key, 9)
    key_collection = jax.random.split(key, 2)
    weak = 0.25 * DK / SEQUENCE_LENGTH * jax.random.uniform(key_collection[0], (SEQUENCE_GROUPS, SEQUENCE_LENGTH, H), minval=rough_lo, maxval=rough_hi)
    strong = jax.random.uniform(key_collection[1], (SEQUENCE_GROUPS, SEQUENCE_LENGTH, H), minval=strong_lo, maxval=strong_hi)
    return jnp.where(fast, strong, weak).astype(jnp.float32).astype(jnp.bfloat16)


def with_ends(array, rng, smallest, top_value):
    place = [jax.random.randint(jax.random.fold_in(rng, axis), (), 0, length) for axis, length in enumerate(array.shape)]
    longest = array.shape.index(max(array.shape))
    neighbour = place[:longest] + [(place[longest] + 1) % array.shape[longest]] + place[longest + 1:]
    return array.at[tuple(place)].set(smallest).at[tuple(neighbour)].set(top_value)


def block_levels(rng, extent, cuts, smallest, largest):
    def one(axis_at, shards_of):
        draws = jax.random.uniform(jax.random.fold_in(jax.random.fold_in(rng, 6), axis_at), (shards_of,), jnp.float32, smallest / len(cuts), largest / len(cuts))
        return jnp.repeat(jnp.exp(draws), extent[axis_at] // shards_of).reshape((-1,) + (1,) * (len(extent) - axis_at - 1))

    loudness = one(*cuts[0])
    for cut in cuts[1:]:
        loudness = loudness * one(*cut)
    return loudness


def bell_draw(stream_key, extent, scale, most, cuts=(), kind=jnp.bfloat16):
    factor_of = block_levels(stream_key, extent, cuts, -0.22, 0.18) if cuts else 1.0
    array = jax.random.normal(stream_key, extent, jnp.float32) * scale * factor_of
    return jnp.minimum(jnp.maximum(array, -most), most).astype(kind)


def setup_inputs(seed: int = 0) -> dict:
    streams_of = jax.random.split(jax.random.key(seed), 9)
    return {
        "queries": bell_draw(streams_of[0], (SEQUENCE_GROUPS, SEQUENCE_LENGTH, HK), 1.0, 6.0, ((0, 4), (1, 32))),
        "keys": bell_draw(streams_of[1], (SEQUENCE_GROUPS, SEQUENCE_LENGTH, HK), 1.0, 6.0, ((0, 4), (1, 32))),
        "values": bell_draw(streams_of[2], (SEQUENCE_GROUPS, SEQUENCE_LENGTH, HK), 1.0, 6.0, ((0, 4), (1, 32))),
        "strength": draw_strength(jax.random.fold_in(streams_of[8], 71), 0),
        "log_decay": draw_log_decay(jax.random.fold_in(streams_of[8], 71), 0),
        "resets": with_ends((jax.random.randint(streams_of[5], (SEQUENCE_GROUPS, SPANS), 0, TOK_DEV * N_SEQ // 128) < 1).astype(jnp.int32), jax.random.fold_in(streams_of[5], 1), 0, 1),
        "out_weight": bell_draw(streams_of[6], (HK, D), HK ** -0.5, 0.1875),
        "cotangent": bell_draw(streams_of[7], (SEQUENCE_GROUPS, SEQUENCE_LENGTH, D), 1.0, 6.0, ((0, 4), (1, 32))),
    }


HIGH = lax.Precision.HIGHEST
EPS = 1e-06

def unit_rows(x):
    return x / jnp.sqrt(lax.optimization_barrier(jnp.sum(x * x, axis=-1, keepdims=True)) + EPS)

def rms_rows(x):
    return x / jnp.sqrt(lax.optimization_barrier(jnp.mean(x * x, axis=-1, keepdims=True)) + EPS)

def to_spans(x, heads, size):
    batch, length = (x.shape[0], x.shape[1])
    parts = x.reshape(batch, length // size, size, heads, -1)
    return parts.transpose(1, 0, 3, 2, 4)

def from_spans(x):
    count, batch, heads, size, width = x.shape
    return x.transpose(1, 0, 3, 2, 4).reshape(batch, count * size, heads * width)

def gates_to_spans(x, size):
    batch, length, heads = x.shape
    return x.reshape(batch, length // size, size, heads).transpose(1, 0, 3, 2)

def block_inverse(keys_n, strength_c, decay_c):
    size = decay_c.shape[-1]
    total = jnp.cumsum(decay_c, axis=-1)
    later = total[..., :, None] - total[..., None, :]
    rows = lax.broadcasted_iota(jnp.int32, (size, size), 0)
    cols = lax.broadcasted_iota(jnp.int32, (size, size), 1)
    below = jnp.where(rows > cols, jnp.exp(jnp.where(rows > cols, later, 0.0)), 0.0)
    key_key = jnp.einsum('...tk,...sk->...ts', keys_n, keys_n, precision=HIGH)
    system = strength_c[..., :, None] * below * key_key
    eye = jnp.eye(size, dtype=decay_c.dtype)
    inverse = eye - system
    power = system
    for level in range(size.bit_length() - 2):
        power = jnp.einsum('...ij,...jk->...ik', power, power, precision=HIGH)
        inverse = inverse + jnp.einsum('...ij,...jk->...ik', inverse, power, precision=HIGH)
    return inverse

def span_step(state, pieces):
    queries, keys_n, values_c, strength_c, decay_c, restart, inverse = pieces
    size = decay_c.shape[-1]
    state = state * (1.0 - restart)[:, None, None, None]
    total = jnp.cumsum(decay_c, axis=-1)
    later = total[..., :, None] - total[..., None, :]
    rows = lax.broadcasted_iota(jnp.int32, (size, size), 0)
    cols = lax.broadcasted_iota(jnp.int32, (size, size), 1)
    inside = jnp.where(rows >= cols, jnp.exp(jnp.where(rows >= cols, later, 0.0)), 0.0)
    growth = jnp.exp(total)
    carried = jnp.einsum('bhtk,bhkv->bhtv', keys_n, state, precision=HIGH)
    target = strength_c[..., None] * (values_c - growth[..., None] * carried)
    deltas = jnp.einsum('bhts,bhsv->bhtv', inverse, target, precision=HIGH)
    query_key = jnp.einsum('bhtk,bhsk->bhts', queries, keys_n, precision=HIGH)
    outputs = growth[..., None] * jnp.einsum('bhtk,bhkv->bhtv', queries, state, precision=HIGH)
    outputs = outputs + jnp.einsum('bhts,bhsv->bhtv', inside * query_key, deltas, precision=HIGH)
    fading = jnp.exp(total[..., -1:] - total)
    new_state = growth[..., -1][..., None, None] * state
    new_state = new_state + jnp.einsum('bhsk,bhsv->bhkv', keys_n * fading[..., None], deltas, precision=HIGH)
    return (new_state, outputs)

def heads_forward(q, k, v, b, g, resets):
    heads = b.shape[-1]
    qn = unit_rows(to_spans(q, heads, SPAN))
    kn = unit_rows(to_spans(k, heads, SPAN))
    vv = to_spans(v, heads, SPAN)
    bb = gates_to_spans(b, SPAN)
    gg = gates_to_spans(g, SPAN)
    restart = resets.T.astype(g.dtype)
    depth = qn.shape[-1]

    def with_inverse(state, pieces):
        inverse = block_inverse(pieces[1], pieces[3], pieces[4])
        return span_step(state, pieces + (inverse,))
    state = jnp.zeros((q.shape[0], heads, depth, vv.shape[-1]), g.dtype)
    final, outs = lax.scan(jax.checkpoint(with_inverse), state, (qn, kn, vv, bb, gg, restart))
    return from_spans(rms_rows(outs))

def reference(queries, keys, values, strength, log_decay, resets, out_weight, cotangent):

    def normed_fn(q, k, v, b, g):
        return heads_forward(q, k, v, b, g, resets)
    normed32, pullback = jax.vjp(normed_fn, queries.astype(jnp.float32), keys.astype(jnp.float32), values.astype(jnp.float32), strength.astype(jnp.float32), log_decay)
    normed = normed32.astype(jnp.bfloat16)
    inner = out_weight.shape[0]
    outer = out_weight.shape[1]
    flat = normed.reshape(-1, inner)
    cot = cotangent.reshape(-1, outer)
    mixed = jnp.dot(flat, out_weight, preferred_element_type=jnp.float32).astype(jnp.bfloat16).reshape(cotangent.shape)
    back = jnp.dot(cot, out_weight.T, preferred_element_type=jnp.float32).reshape(normed32.shape)
    weight_grad = jnp.dot(flat.T, cot, preferred_element_type=jnp.float32) / math.sqrt(flat.shape[0])
    grad_q, grad_k, grad_v, grad_b, grad_g = pullback(back)
    return (mixed, grad_q.astype(jnp.bfloat16), grad_k.astype(jnp.bfloat16), grad_v.astype(jnp.bfloat16), grad_b, grad_g, weight_grad)
```

```python
import math

import jax
import jax.numpy as jnp
from jax import lax
from jax.experimental import pallas as pl
from jax.experimental.pallas import tpu as pltpu
from jax.sharding import PartitionSpec as P

f32 = jnp.float32
bf16 = jnp.bfloat16
EPS = 1e-06
C = 128
H = 8
VMEM_LIMIT = 48 * 1024 * 1024

NN = (((1,), (0,)), ((), ()))
NT = (((1,), (1,)), ((), ()))
TN = (((0,), (0,)), ((), ()))


def split(x):
    hi = x.astype(bf16)
    return hi, (x - hi.astype(f32)).astype(bf16)


def dot(a, b, dims=NN):
    return lax.dot_general(a, b, dims, preferred_element_type=f32)


def mm(a, b, dims=NN):
    ah, al = split(a)
    bh, bl = split(b)
    return dot(ah, bh, dims) + (dot(ah, bl, dims) + dot(al, bh, dims))


def tn(a, b):
    return mm(a.T, b)


def split3(x):
    hi = x.astype(bf16)
    rest = x - hi.astype(f32)
    mid = rest.astype(bf16)
    return hi, mid, (rest - mid.astype(f32)).astype(bf16)


def iotas(shape=(C, C)):
    return lax.broadcasted_iota(jnp.int32, shape, 0), lax.broadcasted_iota(jnp.int32, shape, 1)


def head(ref, h):
    return ref[:, h * C : (h + 1) * C].astype(f32)


def unit(x):
    inv = 1.0 / jnp.sqrt(jnp.sum(x * x, axis=-1, keepdims=True) + EPS)
    return x * inv, inv


def gate_tables(g_ref, resets_ref):
    rows, cols = iotas()
    lower = (rows >= cols).astype(bf16)
    upper = (rows <= cols).astype(bf16)
    parts = split3(g_ref[...])
    total_c = sum(dot(lower, part) for part in parts)
    total_r = sum(dot(part, upper, TN) for part in parts)
    r1 = resets_ref[0, 0].astype(f32)
    r2 = resets_ref[0, 1].astype(f32)
    tcol = lax.broadcasted_iota(jnp.int32, (C, 1), 0)
    m_in = (1.0 - r1) * jnp.where(tcol >= 64, 1.0 - r2, 1.0)
    m_out = jnp.where(tcol >= 64, 1.0, 1.0 - r2)
    m_all = (1.0 - r1) * (1.0 - r2)
    doc = jnp.where((rows >= 64) & (cols < 64), 1.0 - r2, 1.0)
    return total_c, total_r, m_in, m_out, m_all, doc


def head_gates(tables, h):
    total_c, total_r, m_in, m_out, m_all, doc = tables
    rows, cols = iotas()
    tc = total_c[:, h : h + 1]
    tr = total_r[h : h + 1, :]
    last = total_c[C - 1 : C, h : h + 1]
    keep = rows >= cols
    inside = jnp.where(keep, jnp.exp(jnp.where(keep, tc - tr, 0.0)), 0.0) * doc
    growth = jnp.exp(tc) * m_in
    fading = jnp.exp(last - tc) * m_out
    g_last = jnp.exp(last) * m_all
    return inside, growth, fading, g_last


def strict(x):
    rows, cols = iotas()
    return jnp.where(rows > cols, x, 0.0)


def spec_v(n):
    return [pl.BlockSpec(memory_space=pltpu.VMEM)] * n


def spec_s(n):
    return [pl.BlockSpec(memory_space=pltpu.SMEM)] * n


def call(kernel, outs, n_smem, *args, flops=0):
    nbytes = sum(a.size * a.dtype.itemsize for a in args) + sum(
        math.prod(s) * jnp.dtype(d).itemsize for s, d in outs
    )
    return pl.pallas_call(
        kernel,
        out_shape=[jax.ShapeDtypeStruct(s, d) for s, d in outs],
        in_specs=spec_s(n_smem) + spec_v(len(args) - n_smem),
        out_specs=spec_v(len(outs)),
        compiler_params=pltpu.CompilerParams(vmem_limit_bytes=VMEM_LIMIT),
        cost_estimate=pl.CostEstimate(flops=flops, bytes_accessed=nbytes, transcendentals=0),
    )(*args)


HEADS = range(H)
SQ = 2 * C * C * C * 3


def maps_kernel(pos, resets, k_ref, v_ref, b_ref, g_ref, keep_ref, send_ref, inv_ref, uw_ref):
    tables = gate_tables(g_ref, resets)
    rows, cols = iotas()
    eye = (rows == cols).astype(f32)
    block = (rows >= 64) == (cols >= 64)
    beta = b_ref[...].astype(f32)
    kn = [unit(head(k_ref, h))[0] for h in HEADS]
    gates = [head_gates(tables, h) for h in HEADS]
    kk = [mm(kn[h], kn[h], NT) for h in HEADS]
    system = [strict(kk[h] * gates[h][0]) * beta[:, h : h + 1] for h in HEADS]
    near = [jnp.where(block, x, 0.0) for x in system]
    far = [jnp.where(block, 0.0, x) for x in system]
    inv = [eye - x for x in near]
    power = [mm(x, x) for x in near]
    for level in range(5):
        if level < 4:
            both = [mm(jnp.concatenate([inv[h], power[h]], axis=0), power[h]) for h in HEADS]
            inv = [inv[h] + both[h][:C] for h in HEADS]
            power = [both[h][C:] for h in HEADS]
        else:
            inv = [inv[h] + mm(inv[h], power[h]) for h in HEADS]
    cross = [mm(far[h], inv[h]) for h in HEADS]
    inv = [inv[h] - mm(inv[h], cross[h]) for h in HEADS]
    uw = []
    for h in HEADS:
        bh = beta[:, h : h + 1]
        right = jnp.concatenate([kn[h] * (bh * gates[h][1]), head(v_ref, h) * bh], axis=1)
        uw.append(mm(inv[h], right))
    maps = []
    for h in HEADS:
        prod = tn(kn[h] * gates[h][2], uw[h])
        maps.append(
            jnp.concatenate([eye * gates[h][3] - prod[:, :C], prod[:, C:]], axis=1)
        )
    for h in HEADS:
        inv_ref[h] = inv[h]
        uw_ref[h] = uw[h]
    first = pos[3] == 0
    for j in range(4):
        keep_ref[j] = jnp.where(first, maps[j], maps[j + 4])
        send_ref[j] = jnp.where(first, maps[j + 4], maps[j])


def compose(later, earlier):
    moved = mm(later[:, :C], earlier)
    return jnp.concatenate([moved[:, :C], moved[:, C:] + later[:, C:]], axis=1)


def pair_kernel(pos, keep_ref, recv_ref, o0, o1, o2, o3, scratch):
    first = pos[3] == 0
    for j in range(4):
        a, b = keep_ref[j], recv_ref[j]
        early = jnp.where(first, a, b)
        late = jnp.where(first, b, a)
        scratch[j] = compose(late, early)
    for r, out in enumerate((o0, o1, o2, o3)):
        out[...] = scratch[(pos[2] + r) % 4]


def group_kernel(pos, x0, x1, x2, x3, maps_ref, prefix_ref, total_ref):
    for r, ref in enumerate((x0, x1, x2, x3)):
        maps_ref[(pos[2] + 4 - r) % 4] = ref[...]
    run = maps_ref[0]
    prefix_ref[0] = run
    for i in range(1, 4):
        run = compose(maps_ref[i], run)
        if i < 3:
            prefix_ref[i] = run
    total_ref[...] = run


def enter_kernel(pos, t0, t1, t2, t3, prefix_ref, totals_ref, o0, o1, o2, o3, scratch):
    for r, ref in enumerate((t0, t1, t2, t3)):
        totals_ref[(pos[1] + 4 - r) % 4] = ref[...]
    x = pos[1]
    s1 = totals_ref[0, :, C:]
    s2 = mm(totals_ref[1, :, :C], s1) + totals_ref[1, :, C:]
    s3 = mm(totals_ref[2, :, :C], s2) + totals_ref[2, :, C:]
    state = jnp.where(x == 0, 0.0, jnp.where(x == 1, s1, jnp.where(x == 2, s2, s3)))
    scratch[0] = state
    for i in range(3):
        scratch[i + 1] = mm(prefix_ref[i, :, :C], state) + prefix_ref[i, :, C:]
    for r, out in enumerate((o0, o1, o2, o3)):
        out[...] = scratch[(pos[2] + r) % 4]


def split_pair_kernel(pos, s0, s1, s2, s3, keep_ref, recv_ref, mine_ref, other_ref, scratch):
    for r, ref in enumerate((s0, s1, s2, s3)):
        scratch[(pos[2] + 4 - r) % 4] = ref[...]
    first = pos[3] == 0
    for j in range(4):
        early = jnp.where(first, keep_ref[j], recv_ref[j])
        start = scratch[j]
        middle = mm(early[:, :C], start) + early[:, C:]
        mine_ref[j] = jnp.where(first, start, middle)
        other_ref[j] = jnp.where(first, middle, start)


def reads_kernel(resets, q_ref, k_ref, g_ref, uw_ref, read_ref):
    tables = gate_tables(g_ref, resets)
    for h in HEADS:
        qn = unit(head(q_ref, h))[0]
        kn = unit(head(k_ref, h))[0]
        inside, growth, _, _ = head_gates(tables, h)
        attn = mm(qn, kn, NT) * inside
        prod = mm(attn, uw_ref[h])
        read_ref[h] = jnp.concatenate([qn * growth - prod[:, :C], prod[:, C:]], axis=1)


def pick(first, mine_ref, other_ref, h):
    a, b = mine_ref[h % 4], other_ref[h % 4]
    return jnp.where(first, a, b) if h < 4 else jnp.where(first, b, a)


def outs_kernel(
    pos, mine_ref, other_ref, read_ref, dn_ref, n_ref, do_ref, keep_ref, send_ref, c0, c1, c2, c3, wide
):
    first = pos[3] == 0
    reach = []
    for h in HEADS:
        state = pick(first, mine_ref, other_ref, h)
        read = read_ref[h]
        out = mm(read[:, :C], state) + read[:, C:]
        inv = 1.0 / jnp.sqrt(jnp.mean(out * out, axis=-1, keepdims=True) + EPS)
        n32 = out * inv
        n16 = n32.astype(bf16)
        n_ref[:, h * C : (h + 1) * C] = n16
        wide[h // 2, :, (h % 2) * C : (h % 2 + 1) * C] = n16.astype(f32)
        dn = dn_ref[:, h * C : (h + 1) * C]
        do = inv * (dn - n32 * jnp.mean(n32 * dn, axis=-1, keepdims=True))
        do_ref[h] = do
        reach.append(tn(read[:, :C], do))
    for j in range(4):
        keep_ref[j] = jnp.where(first, reach[j], reach[j + 4])
        send_ref[j] = jnp.where(first, reach[j + 4], reach[j])
    for r, out_ref in enumerate((c0, c1, c2, c3)):
        out_ref[...] = wide[(pos[0] + r) % 4]


def pair_back_kernel(pos, keep_ref, recv_ref, mkeep_ref, mrecv_ref, o0, o1, o2, o3, scratch):
    first = pos[3] == 0
    for j in range(4):
        a, b = keep_ref[j], recv_ref[j]
        early = jnp.where(first, a, b)
        late = jnp.where(first, b, a)
        early_map = jnp.where(first, mkeep_ref[j, :, :C], mrecv_ref[j, :, :C])
        scratch[j] = early + tn(early_map, late)
    for r, out in enumerate((o0, o1, o2, o3)):
        out[...] = scratch[(pos[2] + r) % 4]


def group_back_kernel(pos, r0, r1, r2, r3, maps_ref, reach_ref, total_ref):
    for r, ref in enumerate((r0, r1, r2, r3)):
        reach_ref[(pos[2] + 4 - r) % 4] = ref[...]
    run = reach_ref[3]
    for i in (2, 1, 0):
        run = reach_ref[i] + tn(maps_ref[i, :, :C], run)
    total_ref[...] = run


def enter_back_kernel(pos, t0, t1, t2, t3, totals_ref, maps_ref, reach_ref, o0, o1, o2, o3, parts, scratch):
    for r, ref in enumerate((t0, t1, t2, t3)):
        parts[(pos[1] + 4 - r) % 4] = ref[...]
    x = pos[1]
    d2 = parts[3]
    d1 = parts[2] + tn(totals_ref[2, :, :C], d2)
    d0 = parts[1] + tn(totals_ref[1, :, :C], d1)
    run = jnp.where(x == 3, 0.0, jnp.where(x == 2, d2, jnp.where(x == 1, d1, d0)))
    scratch[3] = run
    for i in (2, 1, 0):
        run = reach_ref[i + 1] + tn(maps_ref[i + 1, :, :C], run)
        scratch[i] = run
    for r, out in enumerate((o0, o1, o2, o3)):
        out[...] = scratch[(pos[2] + r) % 4]


def split_pair_back_kernel(
    pos, s0, s1, s2, s3, mkeep_ref, mrecv_ref, keep_ref, recv_ref, mine_ref, other_ref, scratch
):
    for r, ref in enumerate((s0, s1, s2, s3)):
        scratch[(pos[2] + 4 - r) % 4] = ref[...]
    first = pos[3] == 0
    for j in range(4):
        late_map = jnp.where(first, mrecv_ref[j, :, :C], mkeep_ref[j, :, :C])
        late = jnp.where(first, recv_ref[j], keep_ref[j])
        end = scratch[j]
        middle = late + tn(late_map, end)
        mine_ref[j] = jnp.where(first, middle, end)
        other_ref[j] = jnp.where(first, end, middle)


def early_grads_kernel(
    pos, resets, q_ref, k_ref, g_ref, mine_ref, other_ref, uw_ref, do_ref,
    dq_ref, delta_ref, dkn_ref, dd_ref, pair_ref, dgrow_ref,
):
    first = pos[3] == 0
    tables = gate_tables(g_ref, resets)
    for h in HEADS:
        state = pick(first, mine_ref, other_ref, h)
        qn, iq = unit(head(q_ref, h))
        kn = unit(head(k_ref, h))[0]
        inside, growth, _, _ = head_gates(tables, h)
        attn = mm(qn, kn, NT) * inside
        uw = uw_ref[h]
        do = do_ref[h]
        delta = uw[:, C:] - mm(uw[:, :C], state)
        delta_ref[h] = delta
        dattn = mm(do, delta, NT)
        back = mm(do, state, NT)
        pair_ref[h] = dattn * attn
        dgrow_ref[h] = jnp.broadcast_to(
            jnp.sum(back * qn, axis=-1, keepdims=True) * growth, (C, C)
        )
        dqk = dattn * inside
        dqn = back * growth + mm(dqk, kn)
        dq = iq * (dqn - qn * jnp.sum(dqn * qn, axis=-1, keepdims=True))
        dq_ref[:, h * C : (h + 1) * C] = dq.astype(bf16)
        dkn_ref[h] = tn(dqk, qn)
        dd_ref[h] = tn(attn, do)


def late_grads_kernel(
    pos, resets, k_ref, v_ref, b_ref, g_ref, mine_ref, other_ref, dmine_ref, dother_ref,
    inv_ref, delta_ref, dkn_ref, dd_ref, pair_ref, dgrow_ref,
    dk_ref, dv_ref, db_ref, dg_ref,
):
    first = pos[3] == 0
    tables = gate_tables(g_ref, resets)
    rows, cols = iotas()
    beta = b_ref[...].astype(f32)
    db_all = jnp.zeros((C, C), f32)
    dt_all = jnp.zeros((C, C), f32)
    is_last = lax.broadcasted_iota(jnp.int32, (C, 1), 0) == C - 1
    for h in HEADS:
        state = pick(first, mine_ref, other_ref, h)
        dstate = pick(first, dmine_ref, dother_ref, h)
        kn, ik = unit(head(k_ref, h))
        inside, growth, fading, g_last = head_gates(tables, h)
        below = strict(inside)
        bh = beta[:, h : h + 1]
        delta = delta_ref[h]
        ddelta = dd_ref[h] + mm(kn, dstate) * fading
        dtarget = tn(inv_ref[h], ddelta)
        dv_ref[:, h * C : (h + 1) * C] = (dtarget * bh).astype(bf16)
        carried = mm(kn, state)
        db = jnp.sum(dtarget * (head(v_ref, h) - carried * growth), axis=-1, keepdims=True)
        dgrow = -jnp.sum(dtarget * carried, axis=-1, keepdims=True) * bh * growth
        dsys = -mm(dtarget, delta, NT)
        raw = mm(kn, kn, NT) * below
        db = db + jnp.sum(dsys * raw, axis=-1, keepdims=True)
        dkk = dsys * below * bh
        pairs = pair_ref[h] + dsys * raw * bh
        dkf = mm(delta, dstate, NT)
        dfade = jnp.sum(dkf * kn, axis=-1, keepdims=True) * fading
        dkn = (
            dkn_ref[h]
            + mm(dkk + dkk.T, kn)
            + dkf * fading
            - mm(dtarget, state, NT) * (bh * growth)
        )
        dk = ik * (dkn - kn * jnp.sum(dkn * kn, axis=-1, keepdims=True))
        dk_ref[:, h * C : (h + 1) * C] = dk.astype(bf16)
        dlast = jnp.sum(dfade, axis=0, keepdims=True) + g_last * jnp.sum(
            jnp.sum(state * dstate, axis=-1, keepdims=True), axis=0, keepdims=True
        )
        dtotal = (
            jnp.sum(pairs - pairs.T, axis=-1, keepdims=True)
            + dgrow_ref[h][:, :1]
            + dgrow
            - dfade
            + jnp.where(is_last, dlast, 0.0)
        )
        db_all = jnp.where(cols == h, db, db_all)
        dt_all = jnp.where(cols == h, dtotal, dt_all)
    upper = (rows <= cols).astype(bf16)
    dg_all = sum(dot(upper, part) for part in split3(dt_all))
    db_ref[...] = db_all[:, :H]
    dg_ref[...] = dg_all[:, :H]


def wgrad_kernel(pos, n0, n1, n2, n3, cot_ref, keep_ref, send_ref):
    order = [(pos[0] + 4 - r) % 4 for r in range(4)]
    ns = [ref[...].astype(bf16).T for ref in (n0, n1, n2, n3)]
    first = pos[3] == 0
    for j in range(8):
        cols = slice(j * 256, (j + 1) * 256)
        total = sum(
            dot(ns[r], cot_ref[order[r], :, cols].astype(bf16)) for r in range(4)
        ).reshape(16, 2, 8, 256)
        a, b = total[:, 0], total[:, 1]
        keep_ref[:, :, cols] = jnp.where(first, a, b)
        send_ref[:, :, cols] = jnp.where(first, b, a)


def wsum_pair_kernel(pos, keep_ref, recv_ref, o0, o1, o2, o3):
    for r, out in enumerate((o0, o1, o2, o3)):
        z = (pos[2] + r) % 4
        for x in range(4):
            out[x] = keep_ref[4 * x + z] + recv_ref[4 * x + z]


def wsum_z_kernel(pos, a0, a1, a2, a3, o0, o1, o2, o3):
    for r, out in enumerate((o0, o1, o2, o3)):
        x = (pos[1] + r) % 4
        out[...] = (a0[x] + a1[x]) + (a2[x] + a3[x])


def wsum_x_kernel(scale, a0, a1, a2, a3, out):
    out[...] = ((a0[...] + a1[...]) + (a2[...] + a3[...])) * scale


def seq_perm(dx, dz, dc=0):
    pairs = []
    for i in range(32):
        x, z, c = i // 8, (i // 2) % 4, i % 2
        pairs.append((i, ((x + dx) % 4) * 8 + ((z + dz) % 4) * 2 + (c ^ dc)))
    return pairs


def swap_core(x):
    return lax.ppermute(x, "seq", seq_perm(0, 0, 1))


def around_z(parts):
    return [parts[0]] + [lax.ppermute(parts[r], "seq", seq_perm(0, r)) for r in (1, 2, 3)]


def around_x(parts):
    return [parts[0]] + [lax.ppermute(parts[r], "seq", seq_perm(r, 0)) for r in (1, 2, 3)]


def around_dp(parts):
    return [parts[0]] + [
        lax.ppermute(parts[r], "dp", [(i, (i + r) % 4) for i in range(4)]) for r in (1, 2, 3)
    ]


def with_scratch(kernel, outs, n_smem, scratch, *args):
    return pl.pallas_call(
        kernel,
        out_shape=[jax.ShapeDtypeStruct(s, f32) for s in outs],
        in_specs=spec_s(n_smem) + spec_v(len(args) - n_smem),
        out_specs=spec_v(len(outs)),
        scratch_shapes=[pltpu.VMEM(s, f32) for s in scratch],
        compiler_params=pltpu.CompilerParams(vmem_limit_bytes=VMEM_LIMIT),
    )(*args)


def local(queries, keys, values, strength, log_decay, resets, out_weight, cotangent):
    q, k, v = queries[0], keys[0], values[0]
    b, g = strength[0], log_decay[0]
    cot = cotangent[0]
    seq = lax.axis_index("seq")
    pos = jnp.stack([lax.axis_index("dp"), seq // 8, (seq // 2) % 4, seq % 2]).astype(jnp.int32)
    n_all = C * lax.axis_size("seq") * lax.axis_size("dp")

    cots = lax.all_gather(cot.astype(f32), "dp")

    mat, mat2 = (C, C), (C, 2 * C)
    mkeep, msend, inverse, uw = call(
        maps_kernel,
        [((4, *mat2), f32), ((4, *mat2), f32), ((H, *mat), f32), ((H, *mat2), f32)],
        2, pos, resets, k, v, b, g, flops=30 * H * SQ,
    )
    mrecv = swap_core(msend)
    parts = with_scratch(pair_kernel, [mat2] * 4, 1, [(4, *mat2)], pos, mkeep, mrecv)
    parts = around_z(parts)
    dn = lax.dot_general(cot, out_weight, NT, preferred_element_type=f32)
    (reads,) = call(
        reads_kernel, [((H, *mat2), f32)], 1, resets, q, k, g, uw, flops=3 * H * SQ
    )
    maps, prefix, total = call(
        group_kernel, [((4, *mat2), f32), ((3, *mat2), f32), (mat2, f32)], 1, pos, *parts
    )
    parts = around_x([total] * 4)
    totals, *parts = with_scratch(
        enter_kernel, [(4, *mat2)] + [mat] * 4, 1, [(4, *mat)], pos, *parts, prefix
    )
    parts = around_z(parts)
    mine, other = with_scratch(
        split_pair_kernel, [(4, *mat)] * 2, 1, [(4, *mat)], pos, *parts, mkeep, mrecv
    )
    other = swap_core(other)

    n16, do, rkeep, rsend, *chunks = pl.pallas_call(
        outs_kernel,
        out_shape=[
            jax.ShapeDtypeStruct(s, d)
            for s, d in [((C, H * C), bf16), ((H, *mat), f32), ((4, *mat), f32), ((4, *mat), f32)]
            + [(mat2, f32)] * 4
        ],
        in_specs=spec_s(1) + spec_v(4),
        out_specs=spec_v(8),
        scratch_shapes=[pltpu.VMEM((4, *mat2), f32)],
        compiler_params=pltpu.CompilerParams(vmem_limit_bytes=VMEM_LIMIT),
    )(pos, mine, other, reads, dn)

    rrecv = swap_core(rsend)
    parts = with_scratch(
        pair_back_kernel, [mat] * 4, 1, [(4, *mat)], pos, rkeep, rrecv, mkeep, mrecv
    )
    parts = around_z(parts)
    chunks = around_dp(chunks)
    mixed = lax.dot_general(n16, out_weight, NN, preferred_element_type=f32).astype(bf16)
    reach, total = call(
        group_back_kernel, [((4, *mat), f32), (mat, f32)], 1, pos, *parts, maps
    )
    parts = around_x([total] * 4)
    wkeep, wsend = call(
        wgrad_kernel, [((16, 8, 2048), f32)] * 2, 1, pos, *chunks, cots, flops=2 * 512 * 256 * 2048
    )
    dq, delta, dkn, dd, pairs, dgrow = call(
        early_grads_kernel,
        [((C, H * C), bf16)] + [((H, *mat), f32)] * 5,
        2, pos, resets, q, k, g, mine, other, uw, do, flops=8 * H * SQ,
    )
    parts = with_scratch(
        enter_back_kernel, [mat] * 4, 1, [(4, *mat), (4, *mat)], pos, *parts, totals, maps, reach
    )
    parts = around_z(parts)
    dmine, dother = with_scratch(
        split_pair_back_kernel, [(4, *mat)] * 2, 1, [(4, *mat)], pos, *parts, mkeep, mrecv, rkeep, rrecv
    )
    dother = swap_core(dother)
    dk, dv, db, dg = call(
        late_grads_kernel,
        [((C, H * C), bf16), ((C, H * C), bf16), ((C, H), f32), ((C, H), f32)],
        2, pos, resets, k, v, b, g, mine, other, dmine, dother, inverse, delta, dkn, dd, pairs, dgrow,
        flops=8 * H * SQ,
    )

    wrecv = swap_core(wsend)
    wparts = call(wsum_pair_kernel, [((4, 8, 2048), f32)] * 4, 1, pos, wkeep, wrecv)
    wparts = around_z(wparts)
    wparts = call(wsum_z_kernel, [((8, 2048), f32)] * 4, 1, pos, *wparts)
    wparts = around_x(wparts)
    scale = 1.0 / math.sqrt(n_all)

    def last(a0, a1, a2, a3, out):
        wsum_x_kernel(scale, a0, a1, a2, a3, out)

    (weight_grad,) = call(last, [((8, 2048), f32)], 0, *wparts)
    return (mixed[None], dq[None], dk[None], dv[None], db[None], dg[None], weight_grad)


def solution(mesh):
    rows = P("dp", "seq", None)
    return jax.shard_map(
        local,
        mesh=mesh,
        in_specs=(rows, rows, rows, rows, rows, P("dp", "seq"), P(), rows),
        out_specs=(rows, rows, rows, rows, rows, rows, P(("dp", "seq"), None)),
        check_vma=False,
    )
```

```python
import math

import jax
import jax.numpy as jnp
from jax import lax
from jax.experimental import pallas as pl
from jax.experimental.pallas import tpu as pltpu
from jax.sharding import PartitionSpec as P

f32 = jnp.float32
bf16 = jnp.bfloat16
EPS = 1e-06
C = 128
H = 8
VMEM_LIMIT = 48 * 1024 * 1024

NN = (((1,), (0,)), ((), ()))
NT = (((1,), (1,)), ((), ()))
TN = (((0,), (0,)), ((), ()))


def split(x):
    hi = x.astype(bf16)
    return hi, (x - hi.astype(f32)).astype(bf16)


def dot(a, b, dims=NN):
    return lax.dot_general(a, b, dims, preferred_element_type=f32)


def mm(a, b, dims=NN):
    ah, al = split(a)
    bh, bl = split(b)
    left = jnp.concatenate([ah, al], axis=1)
    if dims == NN and b.shape[1] > C:
        return dot(left, jnp.concatenate([bh, bh], axis=0)) + dot(ah, bl)
    n = dims[0][1][0]
    right = jnp.concatenate([bh, bl], axis=1 - n)
    both = dot(left, jnp.concatenate([right, right], axis=n), dims)
    return both[:, :C] + both[:, C:]


def tn(a, b):
    return mm(a.T, b)


def split3(x):
    hi = x.astype(bf16)
    rest = x - hi.astype(f32)
    mid = rest.astype(bf16)
    return hi, mid, (rest - mid.astype(f32)).astype(bf16)


def iotas(shape=(C, C)):
    return lax.broadcasted_iota(jnp.int32, shape, 0), lax.broadcasted_iota(jnp.int32, shape, 1)


def head(ref, h):
    return ref[:, h * C : (h + 1) * C].astype(f32)


def unit(x):
    inv = 1.0 / jnp.sqrt(jnp.sum(x * x, axis=-1, keepdims=True) + EPS)
    return x * inv, inv


def gate_tables(g_ref, resets_ref):
    rows, cols = iotas()
    lower = (rows >= cols).astype(bf16)
    upper = (rows <= cols).astype(bf16)
    parts = split3(g_ref[...])
    total_c = sum(dot(lower, part, NT) for part in parts)
    total_r = sum(dot(part, upper) for part in parts)
    r1 = resets_ref[0, 0].astype(f32)
    r2 = resets_ref[0, 1].astype(f32)
    tcol = lax.broadcasted_iota(jnp.int32, (C, 1), 0)
    m_in = (1.0 - r1) * jnp.where(tcol >= 64, 1.0 - r2, 1.0)
    m_out = jnp.where(tcol >= 64, 1.0, 1.0 - r2)
    m_all = (1.0 - r1) * (1.0 - r2)
    doc = jnp.where((rows >= 64) & (cols < 64), 1.0 - r2, 1.0)
    return total_c, total_r, m_in, m_out, m_all, doc


def head_gates(tables, h):
    total_c, total_r, m_in, m_out, m_all, doc = tables
    rows, cols = iotas()
    tc = total_c[:, h : h + 1]
    tr = total_r[h : h + 1, :]
    last = total_c[C - 1 : C, h : h + 1]
    keep = rows >= cols
    inside = jnp.where(keep, jnp.exp(jnp.where(keep, tc - tr, 0.0)), 0.0) * doc
    growth = jnp.exp(tc) * m_in
    fading = jnp.exp(last - tc) * m_out
    g_last = jnp.exp(last) * m_all
    return inside, growth, fading, g_last


def columns(ref):
    rows, cols = iotas()
    return dot((rows == cols).astype(bf16), ref[...], NT)


def strict(x):
    rows, cols = iotas()
    return jnp.where(rows > cols, x, 0.0)


def spec_v(n):
    return [pl.BlockSpec(memory_space=pltpu.VMEM)] * n


def spec_s(n):
    return [pl.BlockSpec(memory_space=pltpu.SMEM)] * n


def call(kernel, outs, n_smem, *args, flops=0, scratch=(), hbm=0, after=(), limit=VMEM_LIMIT):
    nbytes = sum(a.size * a.dtype.itemsize for a in args) + sum(
        math.prod(s) * jnp.dtype(d).itemsize for s, d in outs
    )
    n_after = len(after)

    def body(*refs):
        kernel(*refs[n_after:])

    in_specs = (
        [pl.BlockSpec(memory_space=pl.ANY)] * n_after
        + spec_s(n_smem)
        + [pl.BlockSpec(memory_space=pltpu.HBM)] * hbm
        + spec_v(len(args) - n_smem - hbm)
    )
    return pl.pallas_call(
        body,
        out_shape=[jax.ShapeDtypeStruct(s, d) for s, d in outs],
        in_specs=in_specs,
        out_specs=spec_v(len(outs)),
        scratch_shapes=list(scratch),
        compiler_params=pltpu.CompilerParams(vmem_limit_bytes=limit),
        cost_estimate=pl.CostEstimate(flops=flops, bytes_accessed=nbytes, transcendentals=0),
    )(*after, *args)


HEADS = range(H)
SQ = 2 * C * C * C * 3


def maps_kernel(
    pos, resets, k_hbm, v_hbm, b_ref, g_ref, keep_ref, send_ref, inv_ref, uw_ref, k_ref, v_ref, sems
):
    load_k = pltpu.make_async_copy(k_hbm, k_ref, sems.at[0])
    load_v = pltpu.make_async_copy(v_hbm, v_ref, sems.at[1])
    load_k.start()
    load_v.start()
    tables = gate_tables(g_ref, resets)
    rows, cols = iotas()
    eye = (rows == cols).astype(f32)
    block = (rows >= 64) == (cols >= 64)
    beta = columns(b_ref)
    gates = [head_gates(tables, h) for h in HEADS]
    load_k.wait()
    kn = [unit(head(k_ref, h))[0] for h in HEADS]
    kk = [mm(kn[h], kn[h], NT) for h in HEADS]
    system = [strict(kk[h] * gates[h][0]) * beta[:, h : h + 1] for h in HEADS]
    near = [jnp.where(block, x, 0.0) for x in system]
    far = [jnp.where(block, 0.0, x) for x in system]
    inv = [eye - x for x in near]
    power = [mm(x, x) for x in near]
    for level in range(5):
        if level < 4:
            both = [mm(jnp.concatenate([inv[h], power[h]], axis=0), power[h]) for h in HEADS]
            inv = [inv[h] + both[h][:C] for h in HEADS]
            power = [both[h][C:] for h in HEADS]
        else:
            inv = [inv[h] + mm(inv[h], power[h]) for h in HEADS]
    cross = [mm(far[h], inv[h]) for h in HEADS]
    inv = [inv[h] - mm(inv[h], cross[h]) for h in HEADS]
    load_v.wait()
    uw = []
    for h in HEADS:
        bh = beta[:, h : h + 1]
        right = jnp.concatenate([kn[h] * (bh * gates[h][1]), head(v_ref, h) * bh], axis=1)
        uw.append(mm(inv[h], right))
    maps = []
    for h in HEADS:
        prod = tn(kn[h] * gates[h][2], uw[h])
        maps.append(
            jnp.concatenate([eye * gates[h][3] - prod[:, :C], prod[:, C:]], axis=1)
        )
    for h in HEADS:
        inv_ref[h] = inv[h]
        uw_ref[h] = uw[h]
    first = pos[3] == 0
    for j in range(4):
        keep_ref[j] = jnp.where(first, maps[j], maps[j + 4])
        send_ref[j] = jnp.where(first, maps[j + 4], maps[j])


def compose(later, earlier):
    moved = mm(later[:, :C], earlier)
    return jnp.concatenate([moved[:, :C], moved[:, C:] + later[:, C:]], axis=1)


def pair_kernel(pos, keep_ref, recv_ref, o0, o1, o2, o3, scratch):
    first = pos[3] == 0
    for j in range(4):
        a, b = keep_ref[j], recv_ref[j]
        early = jnp.where(first, a, b)
        late = jnp.where(first, b, a)
        scratch[j] = compose(late, early)
    for r, out in enumerate((o0, o1, o2, o3)):
        out[...] = scratch[(pos[2] + r) % 4]


def group_kernel(pos, x0, x1, x2, x3, maps_ref, prefix_ref, total_ref):
    for r, ref in enumerate((x0, x1, x2, x3)):
        maps_ref[(pos[2] + 4 - r) % 4] = ref[...]
    run = maps_ref[0]
    prefix_ref[0] = run
    for i in range(1, 4):
        run = compose(maps_ref[i], run)
        if i < 3:
            prefix_ref[i] = run
    total_ref[...] = run


def enter_kernel(pos, t0, t1, t2, t3, prefix_ref, totals_ref, o0, o1, o2, o3, scratch):
    for r, ref in enumerate((t0, t1, t2, t3)):
        totals_ref[(pos[1] + 4 - r) % 4] = ref[...]
    x = pos[1]
    s1 = totals_ref[0, :, C:]
    s2 = mm(totals_ref[1, :, :C], s1) + totals_ref[1, :, C:]
    s3 = mm(totals_ref[2, :, :C], s2) + totals_ref[2, :, C:]
    state = jnp.where(x == 0, 0.0, jnp.where(x == 1, s1, jnp.where(x == 2, s2, s3)))
    scratch[0] = state
    for i in range(3):
        scratch[i + 1] = mm(prefix_ref[i, :, :C], state) + prefix_ref[i, :, C:]
    for r, out in enumerate((o0, o1, o2, o3)):
        out[...] = scratch[(pos[2] + r) % 4]


def split_pair_kernel(pos, s0, s1, s2, s3, keep_ref, recv_ref, mine_ref, other_ref, scratch):
    for r, ref in enumerate((s0, s1, s2, s3)):
        scratch[(pos[2] + 4 - r) % 4] = ref[...]
    first = pos[3] == 0
    for j in range(4):
        early = jnp.where(first, keep_ref[j], recv_ref[j])
        start = scratch[j]
        middle = mm(early[:, :C], start) + early[:, C:]
        mine_ref[j] = jnp.where(first, start, middle)
        other_ref[j] = jnp.where(first, middle, start)


def reads_kernel(resets, q_ref, k_ref, g_ref, uw_ref, read_ref):
    tables = gate_tables(g_ref, resets)
    for h in HEADS:
        qn = unit(head(q_ref, h))[0]
        kn = unit(head(k_ref, h))[0]
        inside, growth, _, _ = head_gates(tables, h)
        attn = mm(qn, kn, NT) * inside
        prod = mm(attn, uw_ref[h])
        read_ref[h] = jnp.concatenate([qn * growth - prod[:, :C], prod[:, C:]], axis=1)


def pick(first, mine_ref, other_ref, h):
    a, b = mine_ref[h % 4], other_ref[h % 4]
    return jnp.where(first, a, b) if h < 4 else jnp.where(first, b, a)


def outs_kernel(
    pos, mine_ref, other_ref, read_ref, dn_ref, n_ref, do_ref, keep_ref, send_ref
):
    first = pos[3] == 0
    reach = []
    for h in HEADS:
        state = pick(first, mine_ref, other_ref, h)
        read = read_ref[h]
        out = mm(read[:, :C], state) + read[:, C:]
        inv = 1.0 / jnp.sqrt(jnp.mean(out * out, axis=-1, keepdims=True) + EPS)
        n32 = out * inv
        n_ref[:, h * C : (h + 1) * C] = n32.astype(bf16)
        dn = dn_ref[:, h * C : (h + 1) * C]
        do = inv * (dn - n32 * jnp.mean(n32 * dn, axis=-1, keepdims=True))
        do_ref[h] = do
        reach.append(tn(read[:, :C], do))
    for j in range(4):
        keep_ref[j] = jnp.where(first, reach[j], reach[j + 4])
        send_ref[j] = jnp.where(first, reach[j + 4], reach[j])


def pair_back_kernel(
    pos, keep_ref, recv_ref, mkeep_ref, mrecv_ref, n_ref, o0, o1, o2, o3, c0, c1, c2, c3, scratch, wide
):
    for j in range(4):
        wide[j] = n_ref[:, 2 * j * C : 2 * (j + 1) * C].astype(f32)
    for r, out_ref in enumerate((c0, c1, c2, c3)):
        out_ref[...] = wide[(pos[0] + r) % 4]
    first = pos[3] == 0
    for j in range(4):
        a, b = keep_ref[j], recv_ref[j]
        early = jnp.where(first, a, b)
        late = jnp.where(first, b, a)
        early_map = jnp.where(first, mkeep_ref[j, :, :C], mrecv_ref[j, :, :C])
        scratch[j] = early + tn(early_map, late)
    for r, out in enumerate((o0, o1, o2, o3)):
        out[...] = scratch[(pos[2] + r) % 4]


def group_back_kernel(pos, r0, r1, r2, r3, maps_ref, reach_ref, total_ref):
    for r, ref in enumerate((r0, r1, r2, r3)):
        reach_ref[(pos[2] + 4 - r) % 4] = ref[...]
    run = reach_ref[3]
    for i in (2, 1, 0):
        run = reach_ref[i] + tn(maps_ref[i, :, :C], run)
    total_ref[...] = run


def enter_back_kernel(pos, t0, t1, t2, t3, totals_ref, maps_ref, reach_ref, o0, o1, o2, o3, parts, scratch):
    for r, ref in enumerate((t0, t1, t2, t3)):
        parts[(pos[1] + 4 - r) % 4] = ref[...]
    x = pos[1]
    d2 = parts[3]
    d1 = parts[2] + tn(totals_ref[2, :, :C], d2)
    d0 = parts[1] + tn(totals_ref[1, :, :C], d1)
    run = jnp.where(x == 3, 0.0, jnp.where(x == 2, d2, jnp.where(x == 1, d1, d0)))
    scratch[3] = run
    for i in (2, 1, 0):
        run = reach_ref[i + 1] + tn(maps_ref[i + 1, :, :C], run)
        scratch[i] = run
    for r, out in enumerate((o0, o1, o2, o3)):
        out[...] = scratch[(pos[2] + r) % 4]


def split_pair_back_kernel(
    pos, s0, s1, s2, s3, mkeep_ref, mrecv_ref, keep_ref, recv_ref, mine_ref, other_ref, scratch
):
    for r, ref in enumerate((s0, s1, s2, s3)):
        scratch[(pos[2] + 4 - r) % 4] = ref[...]
    first = pos[3] == 0
    for j in range(4):
        late_map = jnp.where(first, mrecv_ref[j, :, :C], mkeep_ref[j, :, :C])
        late = jnp.where(first, recv_ref[j], keep_ref[j])
        end = scratch[j]
        middle = late + tn(late_map, end)
        mine_ref[j] = jnp.where(first, middle, end)
        other_ref[j] = jnp.where(first, end, middle)


def early_grads_kernel(
    pos, resets, q_ref, k_ref, g_ref, mine_ref, other_ref, uw_ref, do_ref,
    dq_ref, delta_ref, dkn_ref, dd_ref, pair_ref, dgrow_ref,
):
    first = pos[3] == 0
    tables = gate_tables(g_ref, resets)
    for h in HEADS:
        state = pick(first, mine_ref, other_ref, h)
        qn, iq = unit(head(q_ref, h))
        kn = unit(head(k_ref, h))[0]
        inside, growth, _, _ = head_gates(tables, h)
        attn = mm(qn, kn, NT) * inside
        uw = uw_ref[h]
        do = do_ref[h]
        delta = uw[:, C:] - mm(uw[:, :C], state)
        delta_ref[h] = delta
        dattn = mm(do, delta, NT)
        back = mm(do, state, NT)
        pair_ref[h] = dattn * attn
        dgrow_ref[h] = jnp.broadcast_to(
            jnp.sum(back * qn, axis=-1, keepdims=True) * growth, (C, C)
        )
        dqk = dattn * inside
        dqn = back * growth + mm(dqk, kn)
        dq = iq * (dqn - qn * jnp.sum(dqn * qn, axis=-1, keepdims=True))
        dq_ref[:, h * C : (h + 1) * C] = dq.astype(bf16)
        dkn_ref[h] = tn(dqk, qn)
        dd_ref[h] = tn(attn, do)


def late_grads_kernel(
    pos, resets, k_ref, v_ref, b_ref, g_ref, mine_ref, other_ref, dmine_ref, dother_ref,
    inv_ref, delta_ref, dkn_ref, dd_ref, pair_ref, dgrow_ref,
    dk_ref, dv_ref, db_ref, dg_ref,
):
    first = pos[3] == 0
    tables = gate_tables(g_ref, resets)
    rows, cols = iotas()
    beta = columns(b_ref)
    db_all = jnp.zeros((C, C), f32)
    dt_all = jnp.zeros((C, C), f32)
    is_last = lax.broadcasted_iota(jnp.int32, (C, 1), 0) == C - 1
    for h in HEADS:
        state = pick(first, mine_ref, other_ref, h)
        dstate = pick(first, dmine_ref, dother_ref, h)
        kn, ik = unit(head(k_ref, h))
        inside, growth, fading, g_last = head_gates(tables, h)
        below = strict(inside)
        bh = beta[:, h : h + 1]
        delta = delta_ref[h]
        ddelta = dd_ref[h] + mm(kn, dstate) * fading
        dtarget = tn(inv_ref[h], ddelta)
        dv_ref[:, h * C : (h + 1) * C] = (dtarget * bh).astype(bf16)
        carried = mm(kn, state)
        db = jnp.sum(dtarget * (head(v_ref, h) - carried * growth), axis=-1, keepdims=True)
        dgrow = -jnp.sum(dtarget * carried, axis=-1, keepdims=True) * bh * growth
        dsys = -mm(dtarget, delta, NT)
        raw = mm(kn, kn, NT) * below
        db = db + jnp.sum(dsys * raw, axis=-1, keepdims=True)
        dkk = dsys * below * bh
        pairs = pair_ref[h] + dsys * raw * bh
        dkf = mm(delta, dstate, NT)
        dfade = jnp.sum(dkf * kn, axis=-1, keepdims=True) * fading
        dkn = (
            dkn_ref[h]
            + mm(dkk + dkk.T, kn)
            + dkf * fading
            - mm(dtarget, state, NT) * (bh * growth)
        )
        dk = ik * (dkn - kn * jnp.sum(dkn * kn, axis=-1, keepdims=True))
        dk_ref[:, h * C : (h + 1) * C] = dk.astype(bf16)
        dlast = jnp.sum(dfade, axis=0, keepdims=True) + g_last * jnp.sum(
            jnp.sum(state * dstate, axis=-1, keepdims=True), axis=0, keepdims=True
        )
        dtotal = (
            jnp.sum(pairs - pairs.T, axis=-1, keepdims=True)
            + dgrow_ref[h][:, :1]
            + dgrow
            - dfade
            + jnp.where(is_last, dlast, 0.0)
        )
        db_all = jnp.where(cols == h, db, db_all)
        dt_all = jnp.where(cols == h, dtotal, dt_all)
    lower = (rows >= cols).astype(bf16)
    db_ref[...] = db_all.T[:H]
    dg_ref[...] = sum(dot(part, lower) for part in split3(dt_all.T[:H]))


def widen_kernel(x_ref, o_ref):
    o_ref[...] = x_ref[...].astype(f32)


def relay_kernel(below_ref, above_ref, lower_ref, upper_ref):
    lower_ref[...] = below_ref[:64, :]
    upper_ref[...] = above_ref[64:, :]


def wgrad_kernel(pos, n0, n1, n2, n3, c0, c1, c3, c2_low, c2_up, keep_ref, send_ref):
    ns = [ref[...].astype(bf16).T for ref in (n0, n1, n2, n3)]
    first = pos[3] == 0
    for j in range(8):
        cols = slice(j * 256, (j + 1) * 256)
        far = jnp.concatenate([c2_low[:, cols], c2_up[:, cols]], axis=0)
        cots = (c0[:, cols], c1[:, cols], far, c3[:, cols])
        total = sum(dot(ns[r], cots[r].astype(bf16)) for r in range(4)).reshape(16, 2, 8, 256)
        a, b = total[:, 0], total[:, 1]
        keep_ref[:, :, cols] = jnp.where(first, a, b)
        send_ref[:, :, cols] = jnp.where(first, b, a)


def wsum_pair_kernel(pos, keep_ref, recv_ref, o0, o1, o2, o3):
    for r, out in enumerate((o0, o1, o2, o3)):
        z = (pos[2] + r) % 4
        for x in range(4):
            out[x] = keep_ref[4 * x + z] + recv_ref[4 * x + z]


def wsum_z_kernel(pos, a0, a1, a2, a3, o0, o1, o2, o3):
    for r, out in enumerate((o0, o1, o2, o3)):
        x = (pos[1] + r) % 4
        out[...] = (a0[x] + a1[x]) + (a2[x] + a3[x])


def wsum_x_kernel(scale, a0, a1, a2, a3, out):
    out[...] = ((a0[...] + a1[...]) + (a2[...] + a3[...])) * scale


def seq_perm(dx, dz, dc=0):
    pairs = []
    for i in range(32):
        x, z, c = i // 8, (i // 2) % 4, i % 2
        pairs.append((i, ((x + dx) % 4) * 8 + ((z + dz) % 4) * 2 + (c ^ dc)))
    return pairs


def swap_core(x):
    return lax.ppermute(x, "seq", seq_perm(0, 0, 1))


def around_z(parts):
    return [parts[0]] + [lax.ppermute(parts[r], "seq", seq_perm(0, r)) for r in (1, 2, 3)]


def around_x(parts):
    return [parts[0]] + [lax.ppermute(parts[r], "seq", seq_perm(r, 0)) for r in (1, 2, 3)]


def step_dp(x, r):
    return lax.ppermute(x, "dp", [(i, (i + r) % 4) for i in range(4)])


def around_dp(parts):
    return [parts[0]] + [step_dp(parts[r], r) for r in (1, 2, 3)]


def local(queries, keys, values, strength, log_decay, resets, out_weight, cotangent):
    q, k, v = queries[0], keys[0], values[0]
    b, g = strength[0].T, log_decay[0].T
    cot = cotangent[0]
    seq = lax.axis_index("seq")
    pos = jnp.stack([lax.axis_index("dp"), seq // 8, (seq // 2) % 4, seq % 2]).astype(jnp.int32)
    n_all = C * lax.axis_size("seq") * lax.axis_size("dp")

    mat, mat2 = (C, C), (C, 2 * C)
    one, two = (mat, f32), (mat2, f32)
    four, four2 = ((4, *mat), f32), ((4, *mat2), f32)
    all1, all2 = ((H, *mat), f32), ((H, *mat2), f32)
    wide = ((C, H * C), bf16)
    hold, hold2 = [pltpu.VMEM(*four)], [pltpu.VMEM(*four2)]

    mkeep, msend, inverse, uw = call(
        maps_kernel,
        [four2, four2, all1, all2],
        2, pos, resets, k, v, b, g, flops=30 * H * SQ, hbm=2, limit=62 * 1024 * 1024,
        scratch=[pltpu.VMEM(*wide), pltpu.VMEM(*wide), pltpu.SemaphoreType.DMA((2,))],
    )
    mrecv = swap_core(msend)
    parts = call(pair_kernel, [two] * 4, 1, pos, mkeep, mrecv, scratch=hold2)
    own = parts[0]
    parts = around_z(parts)
    (cot32,) = call(widen_kernel, [((C, 2048), f32)], 0, cot, after=(own,))
    below, above = step_dp(cot32, 1), step_dp(cot32, 3)
    dn = lax.dot_general(cot, out_weight, NT, preferred_element_type=f32)
    maps, prefix, total = call(
        group_kernel, [four2, ((3, *mat2), f32), two], 1, pos, *parts, after=(dn, cot32)
    )
    parts = around_x([total] * 4)
    (reads,) = call(reads_kernel, [all2], 1, resets, q, k, g, uw, flops=3 * H * SQ, after=(total,))
    totals, *parts = call(
        enter_kernel, [four2] + [one] * 4, 1, pos, *parts, prefix, scratch=hold, after=(reads,)
    )
    own = parts[0]
    parts = around_z(parts)
    lower, upper = call(relay_kernel, [((64, 2048), f32)] * 2, 0, below, above, after=(own,))
    lower, upper = step_dp(lower, 1), step_dp(upper, 3)
    mine, other = call(split_pair_kernel, [four] * 2, 1, pos, *parts, mkeep, mrecv, scratch=hold)
    other = swap_core(other)

    n16, do, rkeep, rsend = call(
        outs_kernel, [wide, all1, four, four], 1, pos, mine, other, reads, dn
    )

    rrecv = swap_core(rsend)
    parts = call(
        pair_back_kernel, [one] * 4 + [two] * 4, 1, pos, rkeep, rrecv, mkeep, mrecv, n16,
        scratch=hold + hold2,
    )
    chunks = around_dp(parts[4:])
    parts = around_z(parts[:4])
    mixed = lax.dot_general(n16, out_weight, NN, preferred_element_type=f32).astype(bf16)
    reach, total = call(group_back_kernel, [four, one], 1, pos, *parts, maps, after=(mixed,))
    parts = around_x([total] * 4)
    wkeep, wsend = call(
        wgrad_kernel,
        [((16, 8, 2048), f32)] * 2,
        1, pos, *chunks, cot, below, above, lower, upper, flops=2 * 512 * 256 * 2048, after=(total,),
    )
    wrecv = swap_core(wsend)
    wparts = call(wsum_pair_kernel, [((4, 8, 2048), f32)] * 4, 1, pos, wkeep, wrecv)
    parts = call(
        enter_back_kernel, [one] * 4, 1, pos, *parts, totals, maps, reach, scratch=hold + hold,
        after=(wparts[0],),
    )
    own = parts[0]
    parts = around_z(parts)
    wparts = around_z(wparts)
    dq, delta, dkn, dd, pairs, dgrow = call(
        early_grads_kernel,
        [wide] + [all1] * 5,
        2, pos, resets, q, k, g, mine, other, uw, do, flops=8 * H * SQ, after=(own,),
    )
    dmine, dother = call(
        split_pair_back_kernel, [four] * 2, 1, pos, *parts, mkeep, mrecv, rkeep, rrecv, scratch=hold,
        after=(delta,),
    )
    dother = swap_core(dother)
    wparts = call(wsum_z_kernel, [((8, 2048), f32)] * 4, 1, pos, *wparts, after=(dmine,))
    dk, dv, db, dg = call(
        late_grads_kernel,
        [wide, wide, ((H, C), f32), ((H, C), f32)],
        2, pos, resets, k, v, b, g, mine, other, dmine, dother, inverse, delta, dkn, dd, pairs, dgrow,
        flops=8 * H * SQ, after=(wparts[0],),
    )
    wparts = around_x(wparts)
    scale = 1.0 / math.sqrt(n_all)

    def last(a0, a1, a2, a3, out):
        wsum_x_kernel(scale, a0, a1, a2, a3, out)

    (weight_grad,) = call(last, [((8, 2048), f32)], 0, *wparts, after=(db,))
    return (mixed[None], dq[None], dk[None], dv[None], db.T[None], dg.T[None], weight_grad)


def solution(mesh):
    rows = P("dp", "seq", None)
    return jax.shard_map(
        local,
        mesh=mesh,
        in_specs=(rows, rows, rows, rows, rows, P("dp", "seq"), P(), rows),
        out_specs=(rows, rows, rows, rows, rows, rows, P(("dp", "seq"), None)),
        check_vma=False,
    )
```

```python
import functools
import math

import jax
import jax.numpy as jnp
from jax import lax
from jax.experimental import pallas as pl
from jax.experimental.pallas import tpu as pltpu
from jax.sharding import PartitionSpec as P

f32 = jnp.float32
bf16 = jnp.bfloat16
EPS = 1e-06
C = 128
H = 8
VMEM_LIMIT = 48 * 1024 * 1024
FIRST_LIMIT = 62 * 1024 * 1024

NN = (((1,), (0,)), ((), ()))
NT = (((1,), (1,)), ((), ()))
TN = (((0,), (0,)), ((), ()))


def split(x):
    hi = x.astype(bf16)
    return hi, (x - hi.astype(f32)).astype(bf16)


def dot(a, b, dims=NN):
    return lax.dot_general(a, b, dims, preferred_element_type=f32)


def mm(a, b, dims=NN):
    ah, al = split(a)
    bh, bl = split(b)
    left = jnp.concatenate([ah, al], axis=1)
    n = dims[0][1][0]
    if b.shape[1 - n] > C:
        return dot(left, jnp.concatenate([bh, bh], axis=n), dims) + dot(ah, bl, dims)
    right = jnp.concatenate([bh, bl], axis=1 - n)
    both = dot(left, jnp.concatenate([right, right], axis=n), dims)
    return both[:, :C] + both[:, C:]


def tn(a, b):
    return mm(a.T, b)


def split3(x):
    hi = x.astype(bf16)
    rest = x - hi.astype(f32)
    mid = rest.astype(bf16)
    return hi, mid, (rest - mid.astype(f32)).astype(bf16)


def iotas(shape=(C, C)):
    return lax.broadcasted_iota(jnp.int32, shape, 0), lax.broadcasted_iota(jnp.int32, shape, 1)


def head(ref, h):
    return ref[:, h * C : (h + 1) * C].astype(f32)


def unit(x):
    inv = 1.0 / jnp.sqrt(jnp.sum(x * x, axis=-1, keepdims=True) + EPS)
    return x * inv, inv


def gate_tables(resets, b_ref, g_ref):
    rows, cols = iotas()
    lower = (rows >= cols).astype(bf16)
    upper = (rows <= cols).astype(bf16)
    parts = split3(g_ref[...])
    total_c = sum(dot(lower, part, NT) for part in parts)
    total_r = sum(dot(part, upper) for part in parts)
    beta = dot((rows == cols).astype(bf16), b_ref[...], NT)
    keep1 = 1.0 - resets[0, 0].astype(f32)
    keep2 = 1.0 - resets[0, 1].astype(f32)
    late = lax.broadcasted_iota(jnp.int32, (C, H), 0) >= 64
    growth = jnp.exp(total_c) * (keep1 * jnp.where(late, keep2, 1.0))
    last = total_c[C - 1 : C]
    fading = jnp.exp(last - total_c) * jnp.where(late, 1.0, keep2)
    g_last = jnp.exp(last) * (keep1 * keep2)
    doc = jnp.where((rows >= 64) & (cols < 64), keep2, 1.0)
    return total_c, total_r, growth, fading, g_last, beta, doc


def head_gates(tables, h):
    total_c, total_r, growth, fading, g_last, beta, doc = tables
    rows, cols = iotas()
    keep = rows >= cols
    later = total_c[:, h : h + 1] - total_r[h : h + 1, :]
    inside = jnp.where(keep, jnp.exp(jnp.where(keep, later, 0.0)), 0.0) * doc
    return inside, growth[:, h : h + 1], fading[:, h : h + 1], g_last[:, h : h + 1], beta[:, h : h + 1]


def place():
    seq = lax.axis_index("seq")
    return lax.axis_index("dp"), seq // 8, (seq // 2) % 4, seq % 2


def strict(x):
    rows, cols = iotas()
    return jnp.where(rows > cols, x, 0.0)


def spec_v(n):
    return [pl.BlockSpec(memory_space=pltpu.VMEM)] * n


def call(kernel, outs, n_smem, *args, us=1.0, scratch=(), hbm=(), after=(), limit=VMEM_LIMIT):
    n_after = len(after)

    def body(*refs):
        kernel(*refs[n_after:])

    in_specs = [pl.BlockSpec(memory_space=pl.ANY)] * n_after + [
        pl.BlockSpec(
            memory_space=pltpu.SMEM if i < n_smem else pltpu.HBM if i in hbm else pltpu.VMEM
        )
        for i in range(len(args))
    ]
    return pl.pallas_call(
        body,
        out_shape=[jax.ShapeDtypeStruct(s, d) for s, d in outs],
        in_specs=in_specs,
        out_specs=spec_v(len(outs)),
        scratch_shapes=list(scratch),
        compiler_params=pltpu.CompilerParams(vmem_limit_bytes=limit),
        cost_estimate=pl.CostEstimate(flops=0, bytes_accessed=1, transcendentals=0),
    )(*after, *args)


HEADS = range(H)


def maps_kernel(
    resets, b_ref, g_ref, k_hbm, v_hbm, keep_ref, send_ref, inv_ref, uw_ref, k_ref, v_ref, sems
):
    load_k = pltpu.make_async_copy(k_hbm, k_ref, sems.at[0])
    load_v = pltpu.make_async_copy(v_hbm, v_ref, sems.at[1])
    load_k.start()
    load_v.start()
    tables = gate_tables(resets, b_ref, g_ref)
    rows, cols = iotas()
    eye = (rows == cols).astype(f32)
    block = (rows >= 64) == (cols >= 64)
    gates = [head_gates(tables, h) for h in HEADS]
    load_k.wait()
    kn = [unit(head(k_ref, h))[0] for h in HEADS]
    kk = [mm(kn[h], kn[h], NT) for h in HEADS]
    system = [strict(kk[h] * gates[h][0]) * gates[h][4] for h in HEADS]
    near = [jnp.where(block, x, 0.0) for x in system]
    far = [jnp.where(block, 0.0, x) for x in system]
    inv = [eye - x for x in near]
    power = [mm(x, x) for x in near]
    for level in range(5):
        if level < 4:
            both = [mm(jnp.concatenate([inv[h], power[h]], axis=0), power[h]) for h in HEADS]
            inv = [inv[h] + both[h][:C] for h in HEADS]
            power = [both[h][C:] for h in HEADS]
        else:
            inv = [inv[h] + mm(inv[h], power[h]) for h in HEADS]
    cross = [mm(far[h], inv[h]) for h in HEADS]
    inv = [inv[h] - mm(inv[h], cross[h]) for h in HEADS]
    load_v.wait()
    uw = []
    for h in HEADS:
        bh = gates[h][4]
        right = jnp.concatenate([kn[h] * (bh * gates[h][1]), head(v_ref, h) * bh], axis=1)
        uw.append(mm(inv[h], right))
    maps = []
    for h in HEADS:
        prod = tn(kn[h] * gates[h][2], uw[h])
        maps.append(
            jnp.concatenate([eye * gates[h][3] - prod[:, :C], prod[:, C:]], axis=1)
        )
    for h in HEADS:
        inv_ref[h] = inv[h]
        uw_ref[h] = uw[h]
    first = place()[3] == 0
    for j in range(4):
        keep_ref[j] = jnp.where(first, maps[j], maps[j + 4])
        send_ref[j] = jnp.where(first, maps[j + 4], maps[j])


def compose(later, earlier):
    moved = mm(later[:, :C], earlier)
    return jnp.concatenate([moved[:, :C], moved[:, C:] + later[:, C:]], axis=1)


def pair_kernel(keep_ref, recv_ref, o0, o1, o2, o3, scratch):
    first = place()[3] == 0
    for j in range(4):
        a, b = keep_ref[j], recv_ref[j]
        early = jnp.where(first, a, b)
        late = jnp.where(first, b, a)
        scratch[j] = compose(late, early)
    for r, out in enumerate((o0, o1, o2, o3)):
        out[...] = scratch[(place()[2] + r) % 4]


def group_kernel(x0, x1, x2, x3, maps_ref, prefix_ref, total_ref):
    for r, ref in enumerate((x0, x1, x2, x3)):
        maps_ref[(place()[2] + 4 - r) % 4] = ref[...]
    run = maps_ref[0]
    prefix_ref[0] = run
    for i in range(1, 4):
        run = compose(maps_ref[i], run)
        if i < 3:
            prefix_ref[i] = run
    total_ref[...] = run


def enter_kernel(t0, t1, t2, t3, prefix_ref, totals_ref, o0, o1, o2, o3, scratch):
    for r, ref in enumerate((t0, t1, t2, t3)):
        totals_ref[(place()[1] + 4 - r) % 4] = ref[...]
    x = place()[1]
    s1 = totals_ref[0, :, C:]
    s2 = mm(totals_ref[1, :, :C], s1) + totals_ref[1, :, C:]
    s3 = mm(totals_ref[2, :, :C], s2) + totals_ref[2, :, C:]
    state = jnp.where(x == 0, 0.0, jnp.where(x == 1, s1, jnp.where(x == 2, s2, s3)))
    scratch[0] = state
    for i in range(3):
        scratch[i + 1] = mm(prefix_ref[i, :, :C], state) + prefix_ref[i, :, C:]
    for r, out in enumerate((o0, o1, o2, o3)):
        out[...] = scratch[(place()[2] + r) % 4]


def split_pair_kernel(s0, s1, s2, s3, keep_ref, recv_ref, mine_ref, other_ref, scratch):
    for r, ref in enumerate((s0, s1, s2, s3)):
        scratch[(place()[2] + 4 - r) % 4] = ref[...]
    first = place()[3] == 0
    for j in range(4):
        early = jnp.where(first, keep_ref[j], recv_ref[j])
        start = scratch[j]
        middle = mm(early[:, :C], start) + early[:, C:]
        mine_ref[j] = jnp.where(first, start, middle)
        other_ref[j] = jnp.where(first, middle, start)


def reads_kernel(
    resets, b_ref, g_ref, q_ref, k_ref, uw_ref, inv_ref,
    read_ref, inside_ref, attn_ref, kk_ref, kn_ref, qn_ref, invt_ref,
    growth_ref, fading_ref, beta_ref, iq_ref, ik_ref, last_ref,
):
    tables = gate_tables(resets, b_ref, g_ref)
    growth_ref[...] = tables[2]
    fading_ref[...] = tables[3]
    last_ref[...] = tables[4]
    beta_ref[...] = tables[5]
    cols = lax.broadcasted_iota(jnp.int32, (C, H), 1)
    iq_all = jnp.zeros((C, H), f32)
    ik_all = jnp.zeros((C, H), f32)
    for h in HEADS:
        qn, iq = unit(head(q_ref, h))
        kn, ik = unit(head(k_ref, h))
        inside, growth, _, _, _ = head_gates(tables, h)
        inner = mm(jnp.concatenate([qn, kn], axis=0), kn, NT)
        attn = inner[:C] * inside
        prod = mm(attn, uw_ref[h])
        read_ref[h] = jnp.concatenate([qn * growth - prod[:, :C], prod[:, C:]], axis=1)
        inside_ref[h] = inside
        attn_ref[h] = attn
        kk_ref[h] = inner[C:]
        kn_ref[h] = kn
        qn_ref[h] = qn
        invt_ref[h] = inv_ref[h].T
        iq_all = jnp.where(cols == h, iq, iq_all)
        ik_all = jnp.where(cols == h, ik, ik_all)
    iq_ref[...] = iq_all
    ik_ref[...] = ik_all


def pick(first, mine_ref, other_ref, h):
    a, b = mine_ref[h % 4], other_ref[h % 4]
    return jnp.where(first, a, b) if h < 4 else jnp.where(first, b, a)


def outs_kernel(
    mine_ref, other_ref, read_ref, dn_ref, n_ref, do_ref, keep_ref, send_ref
):
    first = place()[3] == 0
    reach = []
    for h in HEADS:
        state = pick(first, mine_ref, other_ref, h)
        read = read_ref[h]
        out = mm(read[:, :C], state) + read[:, C:]
        inv = 1.0 / jnp.sqrt(jnp.mean(out * out, axis=-1, keepdims=True) + EPS)
        n32 = out * inv
        n_ref[:, h * C : (h + 1) * C] = n32.astype(bf16)
        dn = dn_ref[:, h * C : (h + 1) * C]
        do = inv * (dn - n32 * jnp.mean(n32 * dn, axis=-1, keepdims=True))
        do_ref[h] = do
        reach.append(tn(read[:, :C], do))
    for j in range(4):
        keep_ref[j] = jnp.where(first, reach[j], reach[j + 4])
        send_ref[j] = jnp.where(first, reach[j + 4], reach[j])


def pair_back_kernel(
    keep_ref, recv_ref, mkeep_ref, mrecv_ref, n_ref, o0, o1, o2, o3, c0, c1, c2, c3, scratch, wide
):
    for j in range(4):
        wide[j] = n_ref[:, 2 * j * C : 2 * (j + 1) * C].astype(f32)
    for r, out_ref in enumerate((c0, c1, c2, c3)):
        out_ref[...] = wide[(place()[0] + r) % 4]
    first = place()[3] == 0
    for j in range(4):
        a, b = keep_ref[j], recv_ref[j]
        early = jnp.where(first, a, b)
        late = jnp.where(first, b, a)
        early_map = jnp.where(first, mkeep_ref[j, :, :C], mrecv_ref[j, :, :C])
        scratch[j] = early + tn(early_map, late)
    for r, out in enumerate((o0, o1, o2, o3)):
        out[...] = scratch[(place()[2] + r) % 4]


def group_back_kernel(r0, r1, r2, r3, maps_ref, reach_ref, total_ref):
    for r, ref in enumerate((r0, r1, r2, r3)):
        reach_ref[(place()[2] + 4 - r) % 4] = ref[...]
    run = reach_ref[3]
    for i in (2, 1, 0):
        run = reach_ref[i] + tn(maps_ref[i, :, :C], run)
    total_ref[...] = run


def enter_back_kernel(t0, t1, t2, t3, totals_ref, maps_ref, reach_ref, o0, o1, o2, o3, parts, scratch):
    for r, ref in enumerate((t0, t1, t2, t3)):
        parts[(place()[1] + 4 - r) % 4] = ref[...]
    x = place()[1]
    d2 = parts[3]
    d1 = parts[2] + tn(totals_ref[2, :, :C], d2)
    d0 = parts[1] + tn(totals_ref[1, :, :C], d1)
    run = jnp.where(x == 3, 0.0, jnp.where(x == 2, d2, jnp.where(x == 1, d1, d0)))
    scratch[3] = run
    for i in (2, 1, 0):
        run = reach_ref[i + 1] + tn(maps_ref[i + 1, :, :C], run)
        scratch[i] = run
    for r, out in enumerate((o0, o1, o2, o3)):
        out[...] = scratch[(place()[2] + r) % 4]


def split_pair_back_kernel(
    s0, s1, s2, s3, mkeep_ref, mrecv_ref, keep_ref, recv_ref, mine_ref, other_ref, scratch
):
    for r, ref in enumerate((s0, s1, s2, s3)):
        scratch[(place()[2] + 4 - r) % 4] = ref[...]
    first = place()[3] == 0
    for j in range(4):
        late_map = jnp.where(first, mrecv_ref[j, :, :C], mkeep_ref[j, :, :C])
        late = jnp.where(first, recv_ref[j], keep_ref[j])
        end = scratch[j]
        middle = late + tn(late_map, end)
        mine_ref[j] = jnp.where(first, middle, end)
        other_ref[j] = jnp.where(first, end, middle)


def early_grads_kernel(
    half, mine_ref, other_ref, uw_ref, do_ref, inside_ref, attn_ref, kn_ref, qn_ref, growth_ref, iq_ref, *refs
):
    dq_ref, delta_ref, dkn_ref, dd_ref, carried_ref, rowpart_ref, colpart_ref = refs[half:]
    first = place()[3] == 0
    _, cols = iotas()
    row8 = lax.broadcasted_iota(jnp.int32, (H, C), 0)
    row_all = jnp.zeros((C, C), f32)
    col_all = jnp.zeros((H, C), f32)
    if half:
        dq_ref[:, : 4 * C] = refs[0][...]
    for i in range(4):
        h = 4 * half + i
        state = pick(first, mine_ref, other_ref, h)
        qn, kn, attn = qn_ref[h], kn_ref[h], attn_ref[h]
        uw = uw_ref[h]
        do = do_ref[h]
        moved = mm(jnp.concatenate([uw[:, :C], kn], axis=0), state)
        delta = uw[:, C:] - moved[:C]
        both = mm(do, jnp.concatenate([delta, state], axis=0), NT)
        dattn, back = both[:, :C], both[:, C:] * growth_ref[:, h : h + 1]
        dqk = dattn * inside_ref[h]
        dqn = back + mm(dqk, kn)
        dq = iq_ref[:, h : h + 1] * (dqn - qn * jnp.sum(dqn * qn, axis=-1, keepdims=True))
        dq_ref[:, h * C : (h + 1) * C] = dq.astype(bf16)
        pairs = dattn * attn
        row = jnp.sum(pairs + back * qn, axis=-1, keepdims=True)
        row_all = jnp.where(cols == h, row, row_all)
        col_all = jnp.where(row8 == h, jnp.sum(pairs, axis=0, keepdims=True), col_all)
        dkn_ref[i] = tn(dqk, qn)
        dd_ref[i] = tn(attn, do)
        delta_ref[i] = delta
        carried_ref[i] = moved[C:]
    rowpart_ref[...] = row_all
    colpart_ref[...] = col_all


EARLY = 6


def late_grads_kernel(
    v_ref, mine_ref, other_ref, dmine_ref, dother_ref, inside_ref, kk_ref, kn_ref, invt_ref,
    growth_ref, fading_ref, beta_ref, ik_ref, last_ref, *refs
):
    early = refs[: 2 * EARLY]
    dk_ref, dv_ref, db_ref, dg_ref = refs[2 * EARLY :]
    first = place()[3] == 0
    rows, cols = iotas()
    row8 = lax.broadcasted_iota(jnp.int32, (H, C), 0)
    row_all = early[4][...] + early[EARLY + 4][...]
    col_all = early[5][...] + early[EARLY + 5][...]
    db_all = jnp.zeros((C, C), f32)
    is_last = lax.broadcasted_iota(jnp.int32, (C, 1), 0) == C - 1
    for h in HEADS:
        delta, dkn, dd, carried = (
            ref[h % 4] for ref in early[h // 4 * EARLY : h // 4 * EARLY + 4]
        )
        kk, invt, kn = kk_ref[h], invt_ref[h], kn_ref[h]
        state = pick(first, mine_ref, other_ref, h)
        dstate = pick(first, dmine_ref, dother_ref, h)
        growth, fading, g_last, bh = (
            ref[:, h : h + 1] for ref in (growth_ref, fading_ref, last_ref, beta_ref)
        )
        below = strict(inside_ref[h])
        ddelta = dd + mm(kn, dstate) * fading
        dtarget = mm(invt, ddelta)
        dv_ref[:, h * C : (h + 1) * C] = (dtarget * bh).astype(bf16)
        both = mm(dtarget, jnp.concatenate([delta, state], axis=0), NT)
        dsys, dts = -(both[:, :C] * below), both[:, C:]
        raw = dsys * kk
        dkk = dsys * bh
        dkf = mm(delta, dstate, NT) * fading
        dcar = dtarget * carried * growth
        db = jnp.sum(dtarget * head(v_ref, h) - dcar + raw, axis=-1, keepdims=True)
        pairs = raw * bh
        dfade = dkf * kn
        dlast = jnp.sum(dfade + g_last * (state * dstate), axis=0, keepdims=True)
        dtotal = jnp.sum(pairs - dcar * bh - dfade, axis=-1, keepdims=True)
        dtotal = dtotal + jnp.where(is_last, jnp.sum(dlast, axis=-1, keepdims=True), 0.0)
        dkn = dkn + mm(dkk + dkk.T, kn) + dkf - dts * (bh * growth)
        dk = ik_ref[:, h : h + 1] * (dkn - kn * jnp.sum(dkn * kn, axis=-1, keepdims=True))
        dk_ref[:, h * C : (h + 1) * C] = dk.astype(bf16)
        db_all = jnp.where(cols == h, db, db_all)
        row_all = row_all + jnp.where(cols == h, dtotal, 0.0)
        col_all = col_all + jnp.where(row8 == h, jnp.sum(pairs, axis=0, keepdims=True), 0.0)
    lower = (rows >= cols).astype(bf16)
    db_ref[...] = db_all.T[:H]
    dg_ref[...] = sum(dot(part, lower) for part in split3(row_all.T[:H] - col_all))


def widen_kernel(cot_ref, wide_ref):
    wide_ref[...] = cot_ref[...].astype(f32)


def relay_kernel(below_ref, above_ref, lower_ref, upper_ref):
    lower_ref[...] = below_ref[:64, :]
    upper_ref[...] = above_ref[64:, :]


def wgrad_kernel(n0, n1, n2, n3, c0, c1, c3, c2_low, c2_up, keep_ref, send_ref):
    ns = [ref[...].astype(bf16).T for ref in (n0, n1, n2, n3)]
    first = place()[3] == 0
    for j in range(8):
        cols = slice(j * 256, (j + 1) * 256)
        far = jnp.concatenate([c2_low[:, cols], c2_up[:, cols]], axis=0)
        cots = (c0[:, cols], c1[:, cols], far, c3[:, cols])
        total = sum(dot(ns[r], cots[r].astype(bf16)) for r in range(4)).reshape(16, 2, 8, 256)
        a, b = total[:, 0], total[:, 1]
        keep_ref[:, :, cols] = jnp.where(first, a, b)
        send_ref[:, :, cols] = jnp.where(first, b, a)


def wsum_pair_kernel(keep_ref, recv_ref, o0, o1, o2, o3):
    for r, out in enumerate((o0, o1, o2, o3)):
        z = (place()[2] + r) % 4
        for x in range(4):
            out[x] = keep_ref[4 * x + z] + recv_ref[4 * x + z]


def wsum_z_kernel(a0, a1, a2, a3, o0, o1, o2, o3):
    for r, out in enumerate((o0, o1, o2, o3)):
        x = (place()[1] + r) % 4
        out[...] = (a0[x] + a1[x]) + (a2[x] + a3[x])


def wsum_x_kernel(scale, a0, a1, a2, a3, out):
    out[...] = ((a0[...] + a1[...]) + (a2[...] + a3[...])) * scale


def seq_perm(dx, dz, dc=0):
    pairs = []
    for i in range(32):
        x, z, c = i // 8, (i // 2) % 4, i % 2
        pairs.append((i, ((x + dx) % 4) * 8 + ((z + dz) % 4) * 2 + (c ^ dc)))
    return pairs


def swap_core(x):
    return lax.ppermute(x, "seq", seq_perm(0, 0, 1))


def around_z(parts):
    moved = {r: lax.ppermute(parts[r], "seq", seq_perm(0, r)) for r in (1, 2, 3)}
    return [parts[0], moved[1], moved[2], moved[3]]


def around_x(parts):
    moved = {r: lax.ppermute(parts[r], "seq", seq_perm(r, 0)) for r in (1, 2, 3)}
    return [parts[0], moved[1], moved[2], moved[3]]


def step_dp(x, r):
    return lax.ppermute(x, "dp", [(i, (i + r) % 4) for i in range(4)])


def around_dp(parts):
    moved = {r: step_dp(parts[r], r) for r in (1, 2, 3)}
    return [parts[0], moved[1], moved[2], moved[3]]


def local(queries, keys, values, strength, log_decay, resets, out_weight, cotangent):
    q, k, v = queries[0], keys[0], values[0]
    cot = cotangent[0]
    gates = (resets, strength[0].T, log_decay[0].T)
    n_all = C * lax.axis_size("seq") * lax.axis_size("dp")

    mat, mat2 = (C, C), (C, 2 * C)
    one, two = (mat, f32), (mat2, f32)
    four, four2 = ((4, *mat), f32), ((4, *mat2), f32)
    all1, all2 = ((H, *mat), f32), ((H, *mat2), f32)
    wide = ((C, H * C), bf16)
    hold, hold2 = [pltpu.VMEM(*four)], [pltpu.VMEM(*four2)]

    mkeep, msend, inverse, uw = call(
        maps_kernel,
        [four2, four2, all1, all2],
        1, *gates, k, v, us=6, hbm=(3, 4), limit=FIRST_LIMIT,
        scratch=[pltpu.VMEM(*wide), pltpu.VMEM(*wide), pltpu.SemaphoreType.DMA((2,))],
    )
    mrecv = swap_core(msend)
    parts = call(pair_kernel, [two] * 4, 0, mkeep, mrecv, scratch=hold2)
    own = parts[0]
    parts = around_z(parts)
    (cot32,) = call(widen_kernel, [((C, 2048), f32)], 0, cot, after=(own,))
    dn = lax.dot_general(cot, out_weight, NT, preferred_element_type=f32)
    below, above = step_dp(cot32, 1), step_dp(cot32, 3)
    maps, prefix, total = call(
        group_kernel, [four2, ((3, *mat2), f32), two], 0, *parts, after=(dn, cot32)
    )
    parts = around_x([total] * 4)
    reads, inside, attn, kk, kn, qn, invt, growth, fading, beta, iq, ik, last_decay = call(
        reads_kernel,
        [all2] + [all1] * 6 + [((C, H), f32)] * 5 + [((1, H), f32)],
        1, *gates, q, k, uw, inverse, us=3, after=(total,),
    )
    totals, *parts = call(
        enter_kernel, [four2] + [one] * 4, 0, *parts, prefix, us=1.2, scratch=hold, after=(reads,)
    )
    own = parts[0]
    parts = around_z(parts)
    lower, upper = call(relay_kernel, [((64, 2048), f32)] * 2, 0, below, above, after=(own,))
    lower, upper = step_dp(lower, 1), step_dp(upper, 3)
    mine, other = call(split_pair_kernel, [four] * 2, 0, *parts, mkeep, mrecv, scratch=hold)
    other = swap_core(other)

    n16, do, rkeep, rsend = call(
        outs_kernel, [wide, all1, four, four], 0, mine, other, reads, dn, us=1.6
    )

    rrecv = swap_core(rsend)
    parts = call(
        pair_back_kernel, [one] * 4 + [two] * 4, 0, rkeep, rrecv, mkeep, mrecv, n16,
        scratch=hold + hold2,
    )
    chunks = around_dp(parts[4:])
    own = parts[0]
    parts = around_z(parts[:4])

    def early_grads(half, token, *done):
        return call(
            functools.partial(early_grads_kernel, half),
            [((C, 4 * (1 + half) * C), bf16)] + [four] * 4 + [one, ((H, C), f32)],
            0, mine, other, uw, do, inside, attn, kn, qn, growth, iq, *done, us=2.2, after=(token,),
        )

    early0 = early_grads(0, own)
    mixed = lax.dot_general(n16, out_weight, NN, preferred_element_type=f32).astype(bf16)
    reach, total = call(group_back_kernel, [four, one], 0, *parts, maps, after=(early0[0],))
    parts = around_x([total] * 4)
    wkeep, wsend = call(
        wgrad_kernel,
        [((16, 8, 2048), f32)] * 2,
        0, *chunks, cot, below, above, lower, upper, us=2.5, after=(total,),
    )
    wrecv = swap_core(wsend)
    wparts = call(wsum_pair_kernel, [((4, 8, 2048), f32)] * 4, 0, wkeep, wrecv)
    parts = call(
        enter_back_kernel, [one] * 4, 0, *parts, totals, maps, reach, us=1.5, scratch=hold + hold,
        after=(wparts[0],),
    )
    early1 = early_grads(1, parts[0], early0[0])
    parts = around_z(parts)
    wsent = around_z(wparts)
    dmine, dother = call(
        split_pair_back_kernel, [four] * 2, 0, *parts, mkeep, mrecv, rkeep, rrecv, scratch=hold,
        after=(early1[0], mixed),
    )
    dother = swap_core(dother)
    wparts = call(wsum_z_kernel, [((8, 2048), f32)] * 4, 0, *wsent, after=(dmine,))
    dk, dv, db, dg = call(
        late_grads_kernel,
        [wide, wide, ((H, C), f32), ((H, C), f32)],
        0, v, mine, other, dmine, dother, inside, kk, kn, invt, growth, fading, beta, ik, last_decay,
        *early0[1:], *early1[1:], us=6, after=(wparts[0],),
    )
    wparts = around_x(wparts)
    scale = 1.0 / math.sqrt(n_all)

    def last(a0, a1, a2, a3, out):
        wsum_x_kernel(scale, a0, a1, a2, a3, out)

    (weight_grad,) = call(last, [((8, 2048), f32)], 0, *wparts, after=(db,))
    dq = early1[0]
    return (mixed[None], dq[None], dk[None], dv[None], db.T[None], dg.T[None], weight_grad)


def solution(mesh):
    rows = P("dp", "seq", None)
    return jax.shard_map(
        local,
        mesh=mesh,
        in_specs=(rows, rows, rows, rows, rows, P("dp", "seq"), P(), rows),
        out_specs=(rows, rows, rows, rows, rows, rows, P(("dp", "seq"), None)),
        check_vma=False,
    )
```

```python
import functools
import math

import jax
import jax.numpy as jnp
from jax import lax
from jax.experimental import pallas as pl
from jax.experimental.pallas import tpu as pltpu
from jax.sharding import PartitionSpec as P

f32 = jnp.float32
bf16 = jnp.bfloat16
EPS = 1e-06
C = 128
H = 8
VMEM_LIMIT = 24 * 1024 * 1024
FIRST_LIMIT = 62 * 1024 * 1024

NN = (((1,), (0,)), ((), ()))
NT = (((1,), (1,)), ((), ()))
TN = (((0,), (0,)), ((), ()))


def split(x):
    hi = x.astype(bf16)
    return hi, (x - hi.astype(f32)).astype(bf16)


def dot(a, b, dims=NN):
    return lax.dot_general(a, b, dims, preferred_element_type=f32)


def mm(a, b, dims=NN):
    ah, al = split(a)
    bh, bl = split(b)
    left = jnp.concatenate([ah, al], axis=1)
    n = dims[0][1][0]
    if b.shape[1 - n] > C:
        return dot(left, jnp.concatenate([bh, bh], axis=n), dims) + dot(ah, bl, dims)
    right = jnp.concatenate([bh, bl], axis=1 - n)
    both = dot(left, jnp.concatenate([right, right], axis=n), dims)
    return both[:, :C] + both[:, C:]


def tn(a, b):
    return mm(a.T, b)


def split3(x):
    hi = x.astype(bf16)
    rest = x - hi.astype(f32)
    mid = rest.astype(bf16)
    return hi, mid, (rest - mid.astype(f32)).astype(bf16)


def iotas(shape=(C, C)):
    return lax.broadcasted_iota(jnp.int32, shape, 0), lax.broadcasted_iota(jnp.int32, shape, 1)


def head(ref, h):
    return ref[:, h * C : (h + 1) * C].astype(f32)


def unit(x):
    inv = 1.0 / jnp.sqrt(jnp.sum(x * x, axis=-1, keepdims=True) + EPS)
    return x * inv, inv


def gate_tables(resets, b_ref, g_ref):
    rows, cols = iotas()
    lower = (rows >= cols).astype(bf16)
    upper = (rows <= cols).astype(bf16)
    parts = split3(g_ref[...])
    total_c = sum(dot(lower, part, NT) for part in parts)
    total_r = sum(dot(part, upper) for part in parts)
    beta = dot((rows == cols).astype(bf16), b_ref[...], NT)
    keep1 = 1.0 - resets[0, 0].astype(f32)
    keep2 = 1.0 - resets[0, 1].astype(f32)
    late = lax.broadcasted_iota(jnp.int32, (C, H), 0) >= 64
    growth = jnp.exp(total_c) * (keep1 * jnp.where(late, keep2, 1.0))
    last = total_c[C - 1 : C]
    fading = jnp.exp(last - total_c) * jnp.where(late, 1.0, keep2)
    g_last = jnp.exp(last) * (keep1 * keep2)
    doc = jnp.where((rows >= 64) & (cols < 64), keep2, 1.0)
    return total_c, total_r, growth, fading, g_last, beta, doc


def head_gates(tables, h):
    total_c, total_r, growth, fading, g_last, beta, doc = tables
    rows, cols = iotas()
    keep = rows >= cols
    later = total_c[:, h : h + 1] - total_r[h : h + 1, :]
    inside = jnp.where(keep, jnp.exp(jnp.where(keep, later, 0.0)), 0.0) * doc
    return inside, growth[:, h : h + 1], fading[:, h : h + 1], g_last[:, h : h + 1], beta[:, h : h + 1]


def place():
    seq = lax.axis_index("seq")
    return lax.axis_index("dp"), seq // 8, (seq // 2) % 4, seq % 2


def strict(x):
    rows, cols = iotas()
    return jnp.where(rows > cols, x, 0.0)


def spec_v(n):
    return [pl.BlockSpec(memory_space=pltpu.VMEM)] * n


def call(kernel, outs, n_smem, *args, us=1.0, scratch=(), hbm=(), after=(), limit=VMEM_LIMIT):
    n_after = len(after)

    def body(*refs):
        kernel(*refs[n_after:])

    in_specs = [pl.BlockSpec(memory_space=pl.ANY)] * n_after + [
        pl.BlockSpec(
            memory_space=pltpu.SMEM if i < n_smem else pltpu.HBM if i in hbm else pltpu.VMEM
        )
        for i in range(len(args))
    ]
    return pl.pallas_call(
        body,
        out_shape=[jax.ShapeDtypeStruct(s, d) for s, d in outs],
        in_specs=in_specs,
        out_specs=spec_v(len(outs)),
        scratch_shapes=list(scratch),
        compiler_params=pltpu.CompilerParams(vmem_limit_bytes=limit),
        cost_estimate=pl.CostEstimate(flops=0, bytes_accessed=1, transcendentals=0),
    )(*after, *args)


HEADS = range(H)


def maps_kernel(
    resets, b_ref, g_ref, k_hbm, v_hbm, keep_ref, send_ref, inv_ref, uw_ref, k_ref, v_ref, sems
):
    load_k = pltpu.make_async_copy(k_hbm, k_ref, sems.at[0])
    load_v = pltpu.make_async_copy(v_hbm, v_ref, sems.at[1])
    load_k.start()
    load_v.start()
    tables = gate_tables(resets, b_ref, g_ref)
    rows, cols = iotas()
    eye = (rows == cols).astype(f32)
    block = (rows >= 64) == (cols >= 64)
    gates = [head_gates(tables, h) for h in HEADS]
    load_k.wait()
    kn = [unit(head(k_ref, h))[0] for h in HEADS]
    kk = [mm(kn[h], kn[h], NT) for h in HEADS]
    system = [strict(kk[h] * gates[h][0]) * gates[h][4] for h in HEADS]
    near = [jnp.where(block, x, 0.0) for x in system]
    far = [jnp.where(block, 0.0, x) for x in system]
    inv = [eye - x for x in near]
    power = [mm(x, x) for x in near]
    for level in range(5):
        if level < 4:
            both = [mm(jnp.concatenate([inv[h], power[h]], axis=0), power[h]) for h in HEADS]
            inv = [inv[h] + both[h][:C] for h in HEADS]
            power = [both[h][C:] for h in HEADS]
        else:
            inv = [inv[h] + mm(inv[h], power[h]) for h in HEADS]
    cross = [mm(far[h], inv[h]) for h in HEADS]
    inv = [inv[h] - mm(inv[h], cross[h]) for h in HEADS]
    load_v.wait()
    uw = []
    for h in HEADS:
        bh = gates[h][4]
        right = jnp.concatenate([kn[h] * (bh * gates[h][1]), head(v_ref, h) * bh], axis=1)
        uw.append(mm(inv[h], right))
    maps = []
    for h in HEADS:
        prod = tn(kn[h] * gates[h][2], uw[h])
        maps.append(
            jnp.concatenate([eye * gates[h][3] - prod[:, :C], prod[:, C:]], axis=1)
        )
    for h in HEADS:
        inv_ref[h] = inv[h]
        uw_ref[h] = uw[h]
    first = place()[3] == 0
    for j in range(4):
        keep_ref[j] = jnp.where(first, maps[j], maps[j + 4])
        send_ref[j] = jnp.where(first, maps[j + 4], maps[j])


def compose(later, earlier):
    moved = mm(later[:, :C], earlier)
    return jnp.concatenate([moved[:, :C], moved[:, C:] + later[:, C:]], axis=1)


def pair_kernel(keep_ref, recv_ref, o0, o1, o2, o3, scratch):
    first = place()[3] == 0
    for j in range(4):
        a, b = keep_ref[j], recv_ref[j]
        early = jnp.where(first, a, b)
        late = jnp.where(first, b, a)
        scratch[j] = compose(late, early)
    for r, out in enumerate((o0, o1, o2, o3)):
        out[...] = scratch[(place()[2] + r) % 4]


def group_kernel(x0, x1, x2, x3, maps_ref, prefix_ref, total_ref):
    for r, ref in enumerate((x0, x1, x2, x3)):
        maps_ref[(place()[2] + 4 - r) % 4] = ref[...]
    run = maps_ref[0]
    prefix_ref[0] = run
    for i in range(1, 4):
        run = compose(maps_ref[i], run)
        if i < 3:
            prefix_ref[i] = run
    total_ref[...] = run


def enter_kernel(t0, t1, t2, t3, prefix_ref, totals_ref, o0, o1, o2, o3, scratch):
    for r, ref in enumerate((t0, t1, t2, t3)):
        totals_ref[(place()[1] + 4 - r) % 4] = ref[...]
    x = place()[1]
    s1 = totals_ref[0, :, C:]
    s2 = mm(totals_ref[1, :, :C], s1) + totals_ref[1, :, C:]
    s3 = mm(totals_ref[2, :, :C], s2) + totals_ref[2, :, C:]
    state = jnp.where(x == 0, 0.0, jnp.where(x == 1, s1, jnp.where(x == 2, s2, s3)))
    scratch[0] = state
    for i in range(3):
        scratch[i + 1] = mm(prefix_ref[i, :, :C], state) + prefix_ref[i, :, C:]
    for r, out in enumerate((o0, o1, o2, o3)):
        out[...] = scratch[(place()[2] + r) % 4]


def split_pair_kernel(s0, s1, s2, s3, keep_ref, recv_ref, mine_ref, other_ref, scratch):
    for r, ref in enumerate((s0, s1, s2, s3)):
        scratch[(place()[2] + 4 - r) % 4] = ref[...]
    first = place()[3] == 0
    for j in range(4):
        early = jnp.where(first, keep_ref[j], recv_ref[j])
        start = scratch[j]
        middle = mm(early[:, :C], start) + early[:, C:]
        mine_ref[j] = jnp.where(first, start, middle)
        other_ref[j] = jnp.where(first, middle, start)


def reads_kernel(
    resets, b_ref, g_ref, q_ref, k_ref, uw_ref, inv_ref, mkeep_ref, mrecv_ref,
    read_ref, inside_ref, attn_ref, kk_ref, kn_ref, qn_ref, invt_ref,
    growth_ref, fading_ref, beta_ref, iq_ref, ik_ref, last_ref, early_ref, late_ref,
):
    tables = gate_tables(resets, b_ref, g_ref)
    growth_ref[...] = tables[2]
    fading_ref[...] = tables[3]
    last_ref[...] = tables[4]
    beta_ref[...] = tables[5]
    cols = lax.broadcasted_iota(jnp.int32, (C, H), 1)
    iq_all = jnp.zeros((C, H), f32)
    ik_all = jnp.zeros((C, H), f32)
    for h in HEADS:
        qn, iq = unit(head(q_ref, h))
        kn, ik = unit(head(k_ref, h))
        inside, growth, _, _, _ = head_gates(tables, h)
        inner = mm(jnp.concatenate([qn, kn], axis=0), kn, NT)
        attn = inner[:C] * inside
        prod = mm(attn, uw_ref[h])
        read_ref[h] = jnp.concatenate([qn * growth - prod[:, :C], prod[:, C:]], axis=1)
        inside_ref[h] = inside
        attn_ref[h] = attn
        kk_ref[h] = inner[C:]
        kn_ref[h] = kn
        qn_ref[h] = qn
        invt_ref[h] = inv_ref[h].T
        iq_all = jnp.where(cols == h, iq, iq_all)
        ik_all = jnp.where(cols == h, ik, ik_all)
    first = place()[3] == 0
    for j in range(4):
        a, b = mkeep_ref[j, :, :C], mrecv_ref[j, :, :C]
        early_ref[j] = jnp.where(first, a, b).T
        late_ref[j] = jnp.where(first, b, a).T
    iq_ref[...] = iq_all
    ik_ref[...] = ik_all


def pick(first, mine_ref, other_ref, h):
    a, b = mine_ref[h % 4], other_ref[h % 4]
    return jnp.where(first, a, b) if h < 4 else jnp.where(first, b, a)


def outs_kernel(
    mine_ref, other_ref, read_ref, dn_ref, n_ref, do_ref, keep_ref, send_ref
):
    first = place()[3] == 0
    reach = []
    for h in HEADS:
        state = pick(first, mine_ref, other_ref, h)
        read = read_ref[h]
        out = mm(read[:, :C], state) + read[:, C:]
        inv = 1.0 / jnp.sqrt(jnp.mean(out * out, axis=-1, keepdims=True) + EPS)
        n32 = out * inv
        n_ref[:, h * C : (h + 1) * C] = n32.astype(bf16)
        dn = dn_ref[:, h * C : (h + 1) * C]
        do = inv * (dn - n32 * jnp.mean(n32 * dn, axis=-1, keepdims=True))
        do_ref[h] = do
        reach.append(tn(read[:, :C], do))
    for j in range(4):
        keep_ref[j] = jnp.where(first, reach[j], reach[j + 4])
        send_ref[j] = jnp.where(first, reach[j + 4], reach[j])


def pair_back_kernel(
    keep_ref, recv_ref, early_ref, n_ref, o0, o1, o2, o3, c0, c1, c2, c3, scratch, wide
):
    for j in range(4):
        wide[j] = n_ref[:, 2 * j * C : 2 * (j + 1) * C].astype(f32)
    for r, out_ref in enumerate((c0, c1, c2, c3)):
        out_ref[...] = wide[(place()[0] + r) % 4]
    first = place()[3] == 0
    for j in range(4):
        a, b = keep_ref[j], recv_ref[j]
        early = jnp.where(first, a, b)
        late = jnp.where(first, b, a)
        scratch[j] = early + mm(early_ref[j], late)
    for r, out in enumerate((o0, o1, o2, o3)):
        out[...] = scratch[(place()[2] + r) % 4]


def group_back_kernel(r0, r1, r2, r3, maps_ref, reach_ref, total_ref):
    for r, ref in enumerate((r0, r1, r2, r3)):
        reach_ref[(place()[2] + 4 - r) % 4] = ref[...]
    run = reach_ref[3]
    for i in (2, 1, 0):
        run = reach_ref[i] + tn(maps_ref[i, :, :C], run)
    total_ref[...] = run


def enter_back_kernel(t0, t1, t2, t3, totals_ref, maps_ref, reach_ref, o0, o1, o2, o3, parts, scratch):
    for r, ref in enumerate((t0, t1, t2, t3)):
        parts[(place()[1] + 4 - r) % 4] = ref[...]
    x = place()[1]
    d2 = parts[3]
    d1 = parts[2] + tn(totals_ref[2, :, :C], d2)
    d0 = parts[1] + tn(totals_ref[1, :, :C], d1)
    run = jnp.where(x == 3, 0.0, jnp.where(x == 2, d2, jnp.where(x == 1, d1, d0)))
    scratch[3] = run
    for i in (2, 1, 0):
        run = reach_ref[i + 1] + tn(maps_ref[i + 1, :, :C], run)
        scratch[i] = run
    for r, out in enumerate((o0, o1, o2, o3)):
        out[...] = scratch[(place()[2] + r) % 4]


def split_pair_back_kernel(
    s0, s1, s2, s3, late_ref, keep_ref, recv_ref, mine_ref, other_ref, scratch
):
    for r, ref in enumerate((s0, s1, s2, s3)):
        scratch[(place()[2] + 4 - r) % 4] = ref[...]
    first = place()[3] == 0
    for j in range(4):
        late = jnp.where(first, recv_ref[j], keep_ref[j])
        end = scratch[j]
        middle = late + mm(late_ref[j], end)
        mine_ref[j] = jnp.where(first, middle, end)
        other_ref[j] = jnp.where(first, end, middle)


def early_grads_kernel(
    half, mine_ref, other_ref, uw_ref, do_ref, inside_ref, attn_ref, kn_ref, qn_ref, growth_ref, iq_ref, *refs
):
    dq_ref, delta_ref, dkn_ref, dd_ref, carried_ref, rowpart_ref, colpart_ref = refs[half:]
    first = place()[3] == 0
    _, cols = iotas()
    row8 = lax.broadcasted_iota(jnp.int32, (H, C), 0)
    row_all = jnp.zeros((C, C), f32)
    col_all = jnp.zeros((H, C), f32)
    if half:
        dq_ref[:, : 4 * C] = refs[0][...]
    for i in range(4):
        h = 4 * half + i
        state = pick(first, mine_ref, other_ref, h)
        qn, kn, attn = qn_ref[h], kn_ref[h], attn_ref[h]
        uw = uw_ref[h]
        do = do_ref[h]
        moved = mm(jnp.concatenate([uw[:, :C], kn], axis=0), state)
        delta = uw[:, C:] - moved[:C]
        both = mm(do, jnp.concatenate([delta, state], axis=0), NT)
        dattn, back = both[:, :C], both[:, C:] * growth_ref[:, h : h + 1]
        dqk = dattn * inside_ref[h]
        dqn = back + mm(dqk, kn)
        dq = iq_ref[:, h : h + 1] * (dqn - qn * jnp.sum(dqn * qn, axis=-1, keepdims=True))
        dq_ref[:, h * C : (h + 1) * C] = dq.astype(bf16)
        pairs = dattn * attn
        row = jnp.sum(pairs + back * qn, axis=-1, keepdims=True)
        row_all = jnp.where(cols == h, row, row_all)
        col_all = jnp.where(row8 == h, jnp.sum(pairs, axis=0, keepdims=True), col_all)
        dkn_ref[i] = tn(dqk, qn)
        dd_ref[i] = tn(attn, do)
        delta_ref[i] = delta
        carried_ref[i] = moved[C:]
    rowpart_ref[...] = row_all
    colpart_ref[...] = col_all


EARLY = 6


def late_grads_kernel(
    v_ref, mine_ref, other_ref, dmine_ref, dother_ref, inside_ref, kk_ref, kn_ref, invt_ref,
    growth_ref, fading_ref, beta_ref, ik_ref, last_ref, *refs
):
    early = refs[: 2 * EARLY]
    dk_ref, dv_ref, db_ref, dg_ref, mark_ref = refs[2 * EARLY :]
    first = place()[3] == 0
    rows, cols = iotas()
    row8 = lax.broadcasted_iota(jnp.int32, (H, C), 0)
    row_all = early[4][...] + early[EARLY + 4][...]
    col_all = early[5][...] + early[EARLY + 5][...]
    db_all = jnp.zeros((C, C), f32)
    is_last = lax.broadcasted_iota(jnp.int32, (C, 1), 0) == C - 1
    for h in HEADS:
        delta, dkn, dd, carried = (
            ref[h % 4] for ref in early[h // 4 * EARLY : h // 4 * EARLY + 4]
        )
        kk, invt, kn = kk_ref[h], invt_ref[h], kn_ref[h]
        state = pick(first, mine_ref, other_ref, h)
        dstate = pick(first, dmine_ref, dother_ref, h)
        growth, fading, g_last, bh = (
            ref[:, h : h + 1] for ref in (growth_ref, fading_ref, last_ref, beta_ref)
        )
        below = strict(inside_ref[h])
        ddelta = dd + mm(kn, dstate) * fading
        dtarget = mm(invt, ddelta)
        dv_ref[:, h * C : (h + 1) * C] = (dtarget * bh).astype(bf16)
        both = mm(dtarget, jnp.concatenate([delta, state], axis=0), NT)
        dsys, dts = -(both[:, :C] * below), both[:, C:]
        raw = dsys * kk
        dkk = dsys * bh
        dkf = mm(delta, dstate, NT) * fading
        dcar = dtarget * carried * growth
        db = jnp.sum(dtarget * head(v_ref, h) - dcar + raw, axis=-1, keepdims=True)
        pairs = raw * bh
        dfade = dkf * kn
        dlast = jnp.sum(dfade + g_last * (state * dstate), axis=0, keepdims=True)
        dtotal = jnp.sum(pairs - dcar * bh - dfade, axis=-1, keepdims=True)
        dtotal = dtotal + jnp.where(is_last, jnp.sum(dlast, axis=-1, keepdims=True), 0.0)
        dkn = dkn + mm(dkk + dkk.T, kn) + dkf - dts * (bh * growth)
        dk = ik_ref[:, h : h + 1] * (dkn - kn * jnp.sum(dkn * kn, axis=-1, keepdims=True))
        dk_ref[:, h * C : (h + 1) * C] = dk.astype(bf16)
        db_all = jnp.where(cols == h, db, db_all)
        row_all = row_all + jnp.where(cols == h, dtotal, 0.0)
        col_all = col_all + jnp.where(row8 == h, jnp.sum(pairs, axis=0, keepdims=True), 0.0)
    lower = (rows >= cols).astype(bf16)
    mark_ref[...] = col_all
    db_ref[...] = db_all.T[:H]
    dg_ref[...] = sum(dot(part, lower) for part in split3(row_all.T[:H] - col_all))


def widen_kernel(cot_ref, wide_ref):
    wide_ref[...] = cot_ref[...].astype(f32)


def relay_kernel(below_ref, above_ref, lower_ref, upper_ref):
    lower_ref[...] = below_ref[:64, :]
    upper_ref[...] = above_ref[64:, :]


def wgrad_kernel(n0, n1, n2, n3, c0, c1, c3, c2_low, c2_up, keep_ref, send_ref):
    ns = [ref[...].astype(bf16).T for ref in (n0, n1, n2, n3)]
    first = place()[3] == 0
    for j in range(8):
        cols = slice(j * 256, (j + 1) * 256)
        far = jnp.concatenate([c2_low[:, cols], c2_up[:, cols]], axis=0)
        cots = (c0[:, cols], c1[:, cols], far, c3[:, cols])
        total = sum(dot(ns[r], cots[r].astype(bf16)) for r in range(4)).reshape(16, 2, 8, 256)
        a, b = total[:, 0], total[:, 1]
        keep_ref[:, :, cols] = jnp.where(first, a, b)
        send_ref[:, :, cols] = jnp.where(first, b, a)


def wsum_pair_kernel(keep_ref, recv_ref, o0, o1, o2, o3):
    for r, out in enumerate((o0, o1, o2, o3)):
        x = (place()[1] + r) % 4
        for z in range(4):
            out[z] = keep_ref[4 * x + z] + recv_ref[4 * x + z]


def wsum_first_kernel(a0, a1, a2, a3, o0, o1, o2, o3):
    for r, out in enumerate((o0, o1, o2, o3)):
        z = (place()[2] + r) % 4
        out[...] = (a0[z] + a1[z]) + (a2[z] + a3[z])


def wsum_last_kernel(scale, a0, a1, a2, a3, out):
    out[...] = ((a0[...] + a1[...]) + (a2[...] + a3[...])) * scale


def seq_perm(dx, dz, dc=0):
    pairs = []
    for i in range(32):
        x, z, c = i // 8, (i // 2) % 4, i % 2
        pairs.append((i, ((x + dx) % 4) * 8 + ((z + dz) % 4) * 2 + (c ^ dc)))
    return pairs


def swap_core(x):
    return lax.ppermute(x, "seq", seq_perm(0, 0, 1))


def around_z(parts):
    moved = {r: lax.ppermute(parts[r], "seq", seq_perm(0, r)) for r in (1, 2, 3)}
    return [parts[0], moved[1], moved[2], moved[3]]


def around_x(parts):
    moved = {r: lax.ppermute(parts[r], "seq", seq_perm(r, 0)) for r in (1, 2, 3)}
    return [parts[0], moved[1], moved[2], moved[3]]


def step_dp(x, r):
    return lax.ppermute(x, "dp", [(i, (i + r) % 4) for i in range(4)])


def around_dp(parts):
    moved = {r: step_dp(parts[r], r) for r in (1, 2, 3)}
    return [parts[0], moved[1], moved[2], moved[3]]


def local(queries, keys, values, strength, log_decay, resets, out_weight, cotangent):
    q, k, v = queries[0], keys[0], values[0]
    cot = cotangent[0]
    gates = (resets, strength[0].T, log_decay[0].T)
    n_all = C * lax.axis_size("seq") * lax.axis_size("dp")

    mat, mat2 = (C, C), (C, 2 * C)
    one, two = (mat, f32), (mat2, f32)
    four, four2 = ((4, *mat), f32), ((4, *mat2), f32)
    all1, all2 = ((H, *mat), f32), ((H, *mat2), f32)
    wide = ((C, H * C), bf16)
    hold, hold2 = [pltpu.VMEM(*four)], [pltpu.VMEM(*four2)]

    mkeep, msend, inverse, uw = call(
        maps_kernel,
        [four2, four2, all1, all2],
        1, *gates, k, v, us=6, hbm=(3, 4), limit=FIRST_LIMIT,
        scratch=[pltpu.VMEM(*wide), pltpu.VMEM(*wide), pltpu.SemaphoreType.DMA((2,))],
    )
    mrecv = swap_core(msend)
    parts = call(pair_kernel, [two] * 4, 0, mkeep, mrecv, scratch=hold2)
    own = parts[0]
    parts = around_z(parts)
    (cot32,) = call(widen_kernel, [((C, 2048), f32)], 0, cot, after=(mkeep,))
    dn = lax.dot_general(cot, out_weight, NT, preferred_element_type=f32)
    below, above = step_dp(cot32, 1), step_dp(cot32, 3)
    maps, prefix, total = call(
        group_kernel, [four2, ((3, *mat2), f32), two], 0, *parts, after=(dn, cot32)
    )
    parts = around_x([total] * 4)
    reads, inside, attn, kk, kn, qn, invt, growth, fading, beta, iq, ik, last_decay, early_t, late_t = call(
        reads_kernel,
        [all2] + [all1] * 6 + [((C, H), f32)] * 5 + [((1, H), f32), four, four],
        1, *gates, q, k, uw, inverse, mkeep, mrecv, us=3, after=(total,),
    )
    totals, *parts = call(
        enter_kernel, [four2] + [one] * 4, 0, *parts, prefix, us=1.2, scratch=hold, after=(reads,)
    )
    own = parts[0]
    parts = around_z(parts)
    lower, upper = call(relay_kernel, [((64, 2048), f32)] * 2, 0, below, above, after=(own,))
    lower, upper = step_dp(lower, 1), step_dp(upper, 3)
    mine, other = call(split_pair_kernel, [four] * 2, 0, *parts, mkeep, mrecv, scratch=hold)
    other = swap_core(other)

    n16, do, rkeep, rsend = call(
        outs_kernel, [wide, all1, four, four], 0, mine, other, reads, dn, us=1.6
    )

    rrecv = swap_core(rsend)
    parts = call(
        pair_back_kernel, [one] * 4 + [two] * 4, 0, rkeep, rrecv, early_t, n16,
        scratch=hold + hold2,
    )
    chunks = around_dp(parts[4:])
    own = parts[0]
    parts = around_z(parts[:4])

    def early_grads(half, token, *done):
        return call(
            functools.partial(early_grads_kernel, half),
            [((C, 4 * (1 + half) * C), bf16)] + [four] * 4 + [one, ((H, C), f32)],
            0, mine, other, uw, do, inside, attn, kn, qn, growth, iq, *done, us=2.2, after=(token,),
        )

    early0 = early_grads(0, own)
    mixed = lax.dot_general(n16, out_weight, NN, preferred_element_type=f32).astype(bf16)
    reach, total = call(group_back_kernel, [four, one], 0, *parts, maps)
    parts = around_x([total] * 4)
    early1 = early_grads(1, total, early0[0])
    wkeep, wsend = call(
        wgrad_kernel,
        [((16, 8, 2048), f32)] * 2,
        0, *chunks, cot, below, above, lower, upper, us=2.5, after=(total, early0[0]),
    )
    wrecv = swap_core(wsend)
    wparts = call(wsum_pair_kernel, [((4, 8, 2048), f32)] * 4, 0, wkeep, wrecv)
    parts = call(
        enter_back_kernel, [one] * 4, 0, *parts, totals, maps, reach, us=1.5, scratch=hold + hold,
        after=(wparts[0], early1[1], mixed),
    )
    parts = around_z(parts)
    wsent = around_x(wparts)
    wparts = call(wsum_first_kernel, [((8, 2048), f32)] * 4, 0, *wsent)
    dmine, dother = call(
        split_pair_back_kernel, [four] * 2, 0, *parts, late_t, rkeep, rrecv, scratch=hold,
        after=(wparts[0],),
    )
    dother = swap_core(dother)
    dk, dv, db, dg, mark = call(
        late_grads_kernel,
        [wide, wide, ((H, C), f32), ((H, C), f32), ((H, C), f32)],
        0, v, mine, other, dmine, dother, inside, kk, kn, invt, growth, fading, beta, ik, last_decay,
        *early0[1:], *early1[1:], us=6, after=(wparts[0],),
    )
    wparts = around_z(wparts)
    scale = 1.0 / math.sqrt(n_all)

    def last(a0, a1, a2, a3, out):
        wsum_last_kernel(scale, a0, a1, a2, a3, out)

    (weight_grad,) = call(last, [((8, 2048), f32)], 0, *wparts, after=(mark,))
    dq = early1[0]
    return (mixed[None], dq[None], dk[None], dv[None], db.T[None], dg.T[None], weight_grad)


def solution(mesh):
    rows = P("dp", "seq", None)
    return jax.shard_map(
        local,
        mesh=mesh,
        in_specs=(rows, rows, rows, rows, rows, P("dp", "seq"), P(), rows),
        out_specs=(rows, rows, rows, rows, rows, rows, P(("dp", "seq"), None)),
        check_vma=False,
    )
```

```python
import functools
import math

import jax
import jax.numpy as jnp
from jax import lax
from jax.experimental import pallas as pl
from jax.experimental.pallas import tpu as pltpu
from jax.sharding import PartitionSpec as P

f32 = jnp.float32
bf16 = jnp.bfloat16
EPS = 1e-06
C = 128
H = 8
VMEM_LIMIT = 24 * 1024 * 1024
FIRST_LIMIT = 62 * 1024 * 1024

NN = (((1,), (0,)), ((), ()))
NT = (((1,), (1,)), ((), ()))
TN = (((0,), (0,)), ((), ()))


def split(x):
    hi = x.astype(bf16)
    return hi, (x - hi.astype(f32)).astype(bf16)


def dot(a, b, dims=NN):
    return lax.dot_general(a, b, dims, preferred_element_type=f32)


def mm(a, b, dims=NN):
    ah, al = split(a)
    bh, bl = split(b)
    left = jnp.concatenate([ah, al], axis=1)
    n = dims[0][1][0]
    if b.shape[1 - n] > C:
        return dot(left, jnp.concatenate([bh, bh], axis=n), dims) + dot(ah, bl, dims)
    right = jnp.concatenate([bh, bl], axis=1 - n)
    both = dot(left, jnp.concatenate([right, right], axis=n), dims)
    return both[:, :C] + both[:, C:]


def tn(a, b):
    return mm(a.T, b)


def split3(x):
    hi = x.astype(bf16)
    rest = x - hi.astype(f32)
    mid = rest.astype(bf16)
    return hi, mid, (rest - mid.astype(f32)).astype(bf16)


def iotas(shape=(C, C)):
    return lax.broadcasted_iota(jnp.int32, shape, 0), lax.broadcasted_iota(jnp.int32, shape, 1)


def head(ref, h):
    return ref[:, h * C : (h + 1) * C].astype(f32)


def unit(x):
    inv = 1.0 / jnp.sqrt(jnp.sum(x * x, axis=-1, keepdims=True) + EPS)
    return x * inv, inv


def gate_tables(resets, b_ref, g_ref):
    rows, cols = iotas()
    lower = (rows >= cols).astype(bf16)
    upper = (rows <= cols).astype(bf16)
    parts = split3(g_ref[...])
    total_c = sum(dot(lower, part, NT) for part in parts)
    total_r = sum(dot(part, upper) for part in parts)
    beta = dot((rows == cols).astype(bf16), b_ref[...], NT)
    keep1 = 1.0 - resets[0, 0].astype(f32)
    keep2 = 1.0 - resets[0, 1].astype(f32)
    late = lax.broadcasted_iota(jnp.int32, (C, H), 0) >= 64
    growth = jnp.exp(total_c) * (keep1 * jnp.where(late, keep2, 1.0))
    last = total_c[C - 1 : C]
    fading = jnp.exp(last - total_c) * jnp.where(late, 1.0, keep2)
    g_last = jnp.exp(last) * (keep1 * keep2)
    doc = jnp.where((rows >= 64) & (cols < 64), keep2, 1.0)
    return total_c, total_r, growth, fading, g_last, beta, doc


def head_gates(tables, h):
    total_c, total_r, growth, fading, g_last, beta, doc = tables
    rows, cols = iotas()
    keep = rows >= cols
    later = total_c[:, h : h + 1] - total_r[h : h + 1, :]
    inside = jnp.where(keep, jnp.exp(jnp.where(keep, later, 0.0)), 0.0) * doc
    return inside, growth[:, h : h + 1], fading[:, h : h + 1], g_last[:, h : h + 1], beta[:, h : h + 1]


def place():
    seq = lax.axis_index("seq")
    return lax.axis_index("dp"), seq // 8, (seq // 2) % 4, seq % 2


def strict(x):
    rows, cols = iotas()
    return jnp.where(rows > cols, x, 0.0)


def spec_v(n):
    return [pl.BlockSpec(memory_space=pltpu.VMEM)] * n


def call(kernel, outs, n_smem, *args, us=1.0, scratch=(), hbm=(), after=(), limit=VMEM_LIMIT):
    n_after = len(after)

    def body(*refs):
        kernel(*refs[n_after:])

    in_specs = [pl.BlockSpec(memory_space=pl.ANY)] * n_after + [
        pl.BlockSpec(
            memory_space=pltpu.SMEM if i < n_smem else pltpu.HBM if i in hbm else pltpu.VMEM
        )
        for i in range(len(args))
    ]
    return pl.pallas_call(
        body,
        out_shape=[jax.ShapeDtypeStruct(s, d) for s, d in outs],
        in_specs=in_specs,
        out_specs=spec_v(len(outs)),
        scratch_shapes=list(scratch),
        compiler_params=pltpu.CompilerParams(vmem_limit_bytes=limit),
        cost_estimate=pl.CostEstimate(flops=0, bytes_accessed=1, transcendentals=0),
    )(*after, *args)


HEADS = range(H)


def maps_kernel(
    resets, b_ref, g_ref, k_hbm, v_hbm, cot_hbm, keep_ref, send_ref, inv_ref, uw_ref, wide_ref, k_ref, v_ref, cot_ref, sems
):
    load_k = pltpu.make_async_copy(k_hbm, k_ref, sems.at[0])
    load_v = pltpu.make_async_copy(v_hbm, v_ref, sems.at[1])
    load_cot = pltpu.make_async_copy(cot_hbm, cot_ref, sems.at[2])
    load_k.start()
    load_v.start()
    load_cot.start()
    tables = gate_tables(resets, b_ref, g_ref)
    rows, cols = iotas()
    eye = (rows == cols).astype(f32)
    block = (rows >= 64) == (cols >= 64)
    gates = [head_gates(tables, h) for h in HEADS]
    load_k.wait()
    kn = [unit(head(k_ref, h))[0] for h in HEADS]
    kk = [mm(kn[h], kn[h], NT) for h in HEADS]
    system = [strict(kk[h] * gates[h][0]) * gates[h][4] for h in HEADS]
    near = [jnp.where(block, x, 0.0) for x in system]
    far = [jnp.where(block, 0.0, x) for x in system]
    inv = [eye - x for x in near]
    power = [mm(x, x) for x in near]
    for level in range(5):
        if level < 4:
            both = [mm(jnp.concatenate([inv[h], power[h]], axis=0), power[h]) for h in HEADS]
            inv = [inv[h] + both[h][:C] for h in HEADS]
            power = [both[h][C:] for h in HEADS]
        else:
            inv = [inv[h] + mm(inv[h], power[h]) for h in HEADS]
    cross = [mm(far[h], inv[h]) for h in HEADS]
    inv = [inv[h] - mm(inv[h], cross[h]) for h in HEADS]
    load_cot.wait()
    wide_ref[...] = cot_ref[...].astype(f32)
    load_v.wait()
    uw = []
    for h in HEADS:
        bh = gates[h][4]
        right = jnp.concatenate([kn[h] * (bh * gates[h][1]), head(v_ref, h) * bh], axis=1)
        uw.append(mm(inv[h], right))
    maps = []
    for h in HEADS:
        prod = tn(kn[h] * gates[h][2], uw[h])
        maps.append(
            jnp.concatenate([eye * gates[h][3] - prod[:, :C], prod[:, C:]], axis=1)
        )
    for h in HEADS:
        inv_ref[h] = inv[h]
        uw_ref[h] = uw[h]
    first = place()[3] == 0
    for j in range(4):
        keep_ref[j] = jnp.where(first, maps[j], maps[j + 4])
        send_ref[j] = jnp.where(first, maps[j + 4], maps[j])


def compose(later, earlier):
    moved = mm(later[:, :C], earlier)
    return jnp.concatenate([moved[:, :C], moved[:, C:] + later[:, C:]], axis=1)


def pair_kernel(keep_ref, recv_ref, o0, o1, o2, o3, scratch):
    first = place()[3] == 0
    for j in range(4):
        a, b = keep_ref[j], recv_ref[j]
        early = jnp.where(first, a, b)
        late = jnp.where(first, b, a)
        scratch[j] = compose(late, early)
    for r, out in enumerate((o0, o1, o2, o3)):
        out[...] = scratch[(place()[2] + r) % 4]


def group_kernel(x0, x1, x2, x3, maps_ref, prefix_ref, total_ref):
    for r, ref in enumerate((x0, x1, x2, x3)):
        maps_ref[(place()[2] + 4 - r) % 4] = ref[...]
    run = maps_ref[0]
    prefix_ref[0] = run
    for i in range(1, 4):
        run = compose(maps_ref[i], run)
        if i < 3:
            prefix_ref[i] = run
    total_ref[...] = run


def enter_kernel(t0, t1, t2, t3, prefix_ref, totals_ref, o0, o1, o2, o3, scratch):
    for r, ref in enumerate((t0, t1, t2, t3)):
        totals_ref[(place()[1] + 4 - r) % 4] = ref[...]
    x = place()[1]
    s1 = totals_ref[0, :, C:]
    s2 = mm(totals_ref[1, :, :C], s1) + totals_ref[1, :, C:]
    s3 = mm(totals_ref[2, :, :C], s2) + totals_ref[2, :, C:]
    state = jnp.where(x == 0, 0.0, jnp.where(x == 1, s1, jnp.where(x == 2, s2, s3)))
    scratch[0] = state
    for i in range(3):
        scratch[i + 1] = mm(prefix_ref[i, :, :C], state) + prefix_ref[i, :, C:]
    for r, out in enumerate((o0, o1, o2, o3)):
        out[...] = scratch[(place()[2] + r) % 4]


def split_pair_kernel(s0, s1, s2, s3, keep_ref, recv_ref, mine_ref, other_ref, scratch):
    for r, ref in enumerate((s0, s1, s2, s3)):
        scratch[(place()[2] + 4 - r) % 4] = ref[...]
    first = place()[3] == 0
    for j in range(4):
        early = jnp.where(first, keep_ref[j], recv_ref[j])
        start = scratch[j]
        middle = mm(early[:, :C], start) + early[:, C:]
        mine_ref[j] = jnp.where(first, start, middle)
        other_ref[j] = jnp.where(first, middle, start)


def reads_kernel(
    resets, b_ref, g_ref, q_ref, k_ref, uw_ref, inv_ref, mkeep_ref, mrecv_ref,
    read_ref, inside_ref, attn_ref, kk_ref, kn_ref, qn_ref, invt_ref,
    growth_ref, fading_ref, beta_ref, iq_ref, ik_ref, last_ref, early_ref, late_ref,
):
    tables = gate_tables(resets, b_ref, g_ref)
    growth_ref[...] = tables[2]
    fading_ref[...] = tables[3]
    last_ref[...] = tables[4]
    beta_ref[...] = tables[5]
    cols = lax.broadcasted_iota(jnp.int32, (C, H), 1)
    iq_all = jnp.zeros((C, H), f32)
    ik_all = jnp.zeros((C, H), f32)
    for group in (range(0, 4), range(4, 8)):
        qn, kn, inside, attn = {}, {}, {}, {}
        for h in group:
            qn[h], iq = unit(head(q_ref, h))
            kn[h], ik = unit(head(k_ref, h))
            inside[h], growth, _, _, _ = head_gates(tables, h)
            iq_all = jnp.where(cols == h, iq, iq_all)
            ik_all = jnp.where(cols == h, ik, ik_all)
            inside_ref[h] = inside[h]
            kn_ref[h] = kn[h]
            qn_ref[h] = qn[h]
            invt_ref[h] = inv_ref[h].T
        inner = {h: mm(jnp.concatenate([qn[h], kn[h]], axis=0), kn[h], NT) for h in group}
        for h in group:
            attn[h] = inner[h][:C] * inside[h]
            attn_ref[h] = attn[h]
            kk_ref[h] = inner[h][C:]
        prod = {h: mm(attn[h], uw_ref[h]) for h in group}
        for h in group:
            growth = tables[2][:, h : h + 1]
            read_ref[h] = jnp.concatenate(
                [qn[h] * growth - prod[h][:, :C], prod[h][:, C:]], axis=1
            )
    first = place()[3] == 0
    for j in range(4):
        a, b = mkeep_ref[j, :, :C], mrecv_ref[j, :, :C]
        early_ref[j] = jnp.where(first, a, b).T
        late_ref[j] = jnp.where(first, b, a).T
    iq_ref[...] = iq_all
    ik_ref[...] = ik_all


def pick(first, mine_ref, other_ref, h):
    a, b = mine_ref[h % 4], other_ref[h % 4]
    return jnp.where(first, a, b) if h < 4 else jnp.where(first, b, a)


def outs_kernel(
    mine_ref, other_ref, read_ref, dn_ref, n_ref, do_ref, keep_ref, send_ref
):
    first = place()[3] == 0
    outs = [
        mm(read_ref[h, :, :C], pick(first, mine_ref, other_ref, h)) + read_ref[h, :, C:] for h in HEADS
    ]
    for h in HEADS:
        out = outs[h]
        inv = 1.0 / jnp.sqrt(jnp.mean(out * out, axis=-1, keepdims=True) + EPS)
        n32 = out * inv
        n_ref[:, h * C : (h + 1) * C] = n32.astype(bf16)
        dn = dn_ref[:, h * C : (h + 1) * C]
        do_ref[h] = inv * (dn - n32 * jnp.mean(n32 * dn, axis=-1, keepdims=True))
    reach = [tn(read_ref[h, :, :C], do_ref[h]) for h in HEADS]
    for j in range(4):
        keep_ref[j] = jnp.where(first, reach[j], reach[j + 4])
        send_ref[j] = jnp.where(first, reach[j + 4], reach[j])


def pair_back_kernel(
    keep_ref, recv_ref, early_ref, n_ref, o0, o1, o2, o3, c0, c1, c2, c3, scratch, wide
):
    for j in range(4):
        wide[j] = n_ref[:, 2 * j * C : 2 * (j + 1) * C].astype(f32)
    for r, out_ref in enumerate((c0, c1, c2, c3)):
        out_ref[...] = wide[(place()[0] + r) % 4]
    first = place()[3] == 0
    for j in range(4):
        a, b = keep_ref[j], recv_ref[j]
        early = jnp.where(first, a, b)
        late = jnp.where(first, b, a)
        scratch[j] = early + mm(early_ref[j], late)
    for r, out in enumerate((o0, o1, o2, o3)):
        out[...] = scratch[(place()[2] + r) % 4]


def group_back_kernel(r0, r1, r2, r3, maps_ref, reach_ref, total_ref):
    for r, ref in enumerate((r0, r1, r2, r3)):
        reach_ref[(place()[2] + 4 - r) % 4] = ref[...]
    run = reach_ref[3]
    for i in (2, 1, 0):
        run = reach_ref[i] + tn(maps_ref[i, :, :C], run)
    total_ref[...] = run


def enter_back_kernel(t0, t1, t2, t3, totals_ref, maps_ref, reach_ref, o0, o1, o2, o3, parts, scratch):
    for r, ref in enumerate((t0, t1, t2, t3)):
        parts[(place()[1] + 4 - r) % 4] = ref[...]
    x = place()[1]
    d2 = parts[3]
    d1 = parts[2] + tn(totals_ref[2, :, :C], d2)
    d0 = parts[1] + tn(totals_ref[1, :, :C], d1)
    run = jnp.where(x == 3, 0.0, jnp.where(x == 2, d2, jnp.where(x == 1, d1, d0)))
    scratch[3] = run
    for i in (2, 1, 0):
        run = reach_ref[i + 1] + tn(maps_ref[i + 1, :, :C], run)
        scratch[i] = run
    for r, out in enumerate((o0, o1, o2, o3)):
        out[...] = scratch[(place()[2] + r) % 4]


def split_pair_back_kernel(
    s0, s1, s2, s3, late_ref, keep_ref, recv_ref, mine_ref, other_ref, scratch
):
    for r, ref in enumerate((s0, s1, s2, s3)):
        scratch[(place()[2] + 4 - r) % 4] = ref[...]
    first = place()[3] == 0
    for j in range(4):
        late = jnp.where(first, recv_ref[j], keep_ref[j])
        end = scratch[j]
        middle = late + mm(late_ref[j], end)
        mine_ref[j] = jnp.where(first, middle, end)
        other_ref[j] = jnp.where(first, end, middle)


def early_grads_kernel(
    half, mine_ref, other_ref, uw_ref, do_ref, inside_ref, attn_ref, kn_ref, qn_ref, growth_ref, iq_ref, *refs
):
    dq_ref, delta_ref, dkn_ref, dd_ref, carried_ref, rowpart_ref, colpart_ref = refs[half:]
    first = place()[3] == 0
    _, cols = iotas()
    row8 = lax.broadcasted_iota(jnp.int32, (H, C), 0)
    row_all = jnp.zeros((C, C), f32)
    col_all = jnp.zeros((H, C), f32)
    if half:
        dq_ref[:, : 4 * C] = refs[0][...]
    group = range(4 * half, 4 * half + 4)
    state = {h: pick(first, mine_ref, other_ref, h) for h in group}
    moved = {
        h: mm(jnp.concatenate([uw_ref[h, :, :C], kn_ref[h]], axis=0), state[h]) for h in group
    }
    delta = {h: uw_ref[h, :, C:] - moved[h][:C] for h in group}
    for h in group:
        dd_ref[h % 4] = tn(attn_ref[h], do_ref[h])
        delta_ref[h % 4] = delta[h]
        carried_ref[h % 4] = moved[h][C:]
    both = {
        h: mm(do_ref[h], jnp.concatenate([delta[h], state[h]], axis=0), NT) for h in group
    }
    dqk = {h: both[h][:, :C] * inside_ref[h] for h in group}
    back = {h: both[h][:, C:] * growth_ref[:, h : h + 1] for h in group}
    dqn = {h: back[h] + mm(dqk[h], kn_ref[h]) for h in group}
    for h in group:
        dkn_ref[h % 4] = tn(dqk[h], qn_ref[h])
    for h in group:
        qn = qn_ref[h]
        dq = iq_ref[:, h : h + 1] * (
            dqn[h] - qn * jnp.sum(dqn[h] * qn, axis=-1, keepdims=True)
        )
        dq_ref[:, h * C : (h + 1) * C] = dq.astype(bf16)
        pairs = both[h][:, :C] * attn_ref[h]
        row = jnp.sum(pairs + back[h] * qn, axis=-1, keepdims=True)
        row_all = jnp.where(cols == h, row, row_all)
        col_all = jnp.where(row8 == h, jnp.sum(pairs, axis=0, keepdims=True), col_all)
    rowpart_ref[...] = row_all
    colpart_ref[...] = col_all


EARLY = 6


def late_grads_kernel(
    v_ref, mine_ref, other_ref, dmine_ref, dother_ref, inside_ref, kk_ref, kn_ref, invt_ref,
    growth_ref, fading_ref, beta_ref, ik_ref, last_ref, *refs
):
    early = refs[: 2 * EARLY]
    dk_ref, dv_ref, db_ref, dg_ref, mark_ref = refs[2 * EARLY :]
    first = place()[3] == 0
    rows, cols = iotas()
    row8 = lax.broadcasted_iota(jnp.int32, (H, C), 0)
    row_all = early[4][...] + early[EARLY + 4][...]
    col_all = early[5][...] + early[EARLY + 5][...]
    db_all = jnp.zeros((C, C), f32)
    is_last = lax.broadcasted_iota(jnp.int32, (C, 1), 0) == C - 1
    for group in (range(0, 4), range(4, 8)):
        delta, dkn, dd, carried = (
            {h: early[h // 4 * EARLY + part][h % 4] for h in group} for part in range(4)
        )
        state = {h: pick(first, mine_ref, other_ref, h) for h in group}
        dstate = {h: pick(first, dmine_ref, dother_ref, h) for h in group}
        growth, fading, g_last, bh = (
            {h: ref[:, h : h + 1] for h in group} for ref in (growth_ref, fading_ref, last_ref, beta_ref)
        )
        ddelta = {h: dd[h] + mm(kn_ref[h], dstate[h]) * fading[h] for h in group}
        dkf = {h: mm(delta[h], dstate[h], NT) * fading[h] for h in group}
        dtarget = {h: mm(invt_ref[h], ddelta[h]) for h in group}
        both = {
            h: mm(dtarget[h], jnp.concatenate([delta[h], state[h]], axis=0), NT) for h in group
        }
        dsys = {h: -(both[h][:, :C] * strict(inside_ref[h])) for h in group}
        dkk = {h: dsys[h] * bh[h] for h in group}
        inner = {h: mm(dkk[h] + dkk[h].T, kn_ref[h]) for h in group}
        for h in group:
            dv_ref[:, h * C : (h + 1) * C] = (dtarget[h] * bh[h]).astype(bf16)
            raw = dsys[h] * kk_ref[h]
            dcar = dtarget[h] * carried[h] * growth[h]
            db = jnp.sum(dtarget[h] * head(v_ref, h) - dcar + raw, axis=-1, keepdims=True)
            pairs = raw * bh[h]
            dfade = dkf[h] * kn_ref[h]
            dlast = jnp.sum(dfade + g_last[h] * (state[h] * dstate[h]), axis=0, keepdims=True)
            dtotal = jnp.sum(pairs - dcar * bh[h] - dfade, axis=-1, keepdims=True)
            dtotal = dtotal + jnp.where(is_last, jnp.sum(dlast, axis=-1, keepdims=True), 0.0)
            grad = dkn[h] + inner[h] + dkf[h] - both[h][:, C:] * (bh[h] * growth[h])
            dk = ik_ref[:, h : h + 1] * (
                grad - kn_ref[h] * jnp.sum(grad * kn_ref[h], axis=-1, keepdims=True)
            )
            dk_ref[:, h * C : (h + 1) * C] = dk.astype(bf16)
            db_all = jnp.where(cols == h, db, db_all)
            row_all = row_all + jnp.where(cols == h, dtotal, 0.0)
            col_all = col_all + jnp.where(row8 == h, jnp.sum(pairs, axis=0, keepdims=True), 0.0)
    lower = (rows >= cols).astype(bf16)
    mark_ref[...] = col_all
    db_ref[...] = db_all.T[:H]
    dg_ref[...] = sum(dot(part, lower) for part in split3(row_all.T[:H] - col_all))


def relay_kernel(below_ref, above_ref, lower_ref, upper_ref):
    lower_ref[...] = below_ref[:64, :]
    upper_ref[...] = above_ref[64:, :]


def wgrad_kernel(n0, n1, n2, n3, c0, c1, c3, c2_low, c2_up, keep_ref, send_ref):
    ns = [ref[...].astype(bf16).T for ref in (n0, n1, n2, n3)]
    first = place()[3] == 0
    for j in range(8):
        cols = slice(j * 256, (j + 1) * 256)
        far = jnp.concatenate([c2_low[:, cols], c2_up[:, cols]], axis=0)
        cots = (c0[:, cols], c1[:, cols], far, c3[:, cols])
        total = sum(dot(ns[r], cots[r].astype(bf16)) for r in range(4)).reshape(16, 2, 8, 256)
        a, b = total[:, 0], total[:, 1]
        keep_ref[:, :, cols] = jnp.where(first, a, b)
        send_ref[:, :, cols] = jnp.where(first, b, a)


def wsum_pair_kernel(keep_ref, recv_ref, o0, o1, o2, o3):
    for r, out in enumerate((o0, o1, o2, o3)):
        x = (place()[1] + r) % 4
        for z in range(4):
            out[z] = keep_ref[4 * x + z] + recv_ref[4 * x + z]


def wsum_first_kernel(a0, a1, a2, a3, o0, o1, o2, o3):
    for r, out in enumerate((o0, o1, o2, o3)):
        z = (place()[2] + r) % 4
        out[...] = (a0[z] + a1[z]) + (a2[z] + a3[z])


def wsum_last_kernel(scale, a0, a1, a2, a3, out):
    out[...] = ((a0[...] + a1[...]) + (a2[...] + a3[...])) * scale


def seq_perm(dx, dz, dc=0):
    pairs = []
    for i in range(32):
        x, z, c = i // 8, (i // 2) % 4, i % 2
        pairs.append((i, ((x + dx) % 4) * 8 + ((z + dz) % 4) * 2 + (c ^ dc)))
    return pairs


def swap_core(x):
    return lax.ppermute(x, "seq", seq_perm(0, 0, 1))


def around_z(parts):
    moved = {r: lax.ppermute(parts[r], "seq", seq_perm(0, r)) for r in (1, 2, 3)}
    return [parts[0], moved[1], moved[2], moved[3]]


def around_x(parts):
    moved = {r: lax.ppermute(parts[r], "seq", seq_perm(r, 0)) for r in (1, 2, 3)}
    return [parts[0], moved[1], moved[2], moved[3]]


def step_dp(x, r):
    return lax.ppermute(x, "dp", [(i, (i + r) % 4) for i in range(4)])


def around_dp(parts):
    moved = {r: step_dp(parts[r], r) for r in (2, 1, 3)}
    return [parts[0], moved[1], moved[2], moved[3]]


def local(queries, keys, values, strength, log_decay, resets, out_weight, cotangent):
    q, k, v = queries[0], keys[0], values[0]
    cot = cotangent[0]
    gates = (resets, strength[0].T, log_decay[0].T)
    n_all = C * lax.axis_size("seq") * lax.axis_size("dp")

    mat, mat2 = (C, C), (C, 2 * C)
    one, two = (mat, f32), (mat2, f32)
    four, four2 = ((4, *mat), f32), ((4, *mat2), f32)
    all1, all2 = ((H, *mat), f32), ((H, *mat2), f32)
    wide = ((C, H * C), bf16)
    hold, hold2 = [pltpu.VMEM(*four)], [pltpu.VMEM(*four2)]

    mkeep, msend, inverse, uw, cot32 = call(
        maps_kernel,
        [four2, four2, all1, all2, ((C, 2048), f32)],
        1, *gates, k, v, cot, us=6, hbm=(3, 4, 5), limit=FIRST_LIMIT,
        scratch=[
            pltpu.VMEM(*wide), pltpu.VMEM(*wide), pltpu.VMEM((C, 2048), bf16), pltpu.SemaphoreType.DMA((3,)),
        ],
    )
    mrecv = swap_core(msend)
    parts = call(pair_kernel, [two] * 4, 0, mkeep, mrecv, scratch=hold2)
    own = parts[0]
    parts = around_z(parts)
    dn = lax.dot_general(cot, out_weight, NT, preferred_element_type=f32)
    below, above = step_dp(cot32, 1), step_dp(cot32, 3)
    maps, prefix, total = call(
        group_kernel, [four2, ((3, *mat2), f32), two], 0, *parts, after=(dn, cot32)
    )
    parts = around_x([total] * 4)
    reads, inside, attn, kk, kn, qn, invt, growth, fading, beta, iq, ik, last_decay, early_t, late_t = call(
        reads_kernel,
        [all2] + [all1] * 6 + [((C, H), f32)] * 5 + [((1, H), f32), four, four],
        1, *gates, q, k, uw, inverse, mkeep, mrecv, us=3, after=(total,),
    )
    totals, *parts = call(
        enter_kernel, [four2] + [one] * 4, 0, *parts, prefix, us=1.2, scratch=hold, after=(reads,)
    )
    own = parts[0]
    parts = around_z(parts)
    lower, upper = call(relay_kernel, [((64, 2048), f32)] * 2, 0, below, above, after=(own,))
    lower, upper = step_dp(lower, 1), step_dp(upper, 3)
    mine, other = call(split_pair_kernel, [four] * 2, 0, *parts, mkeep, mrecv, scratch=hold)
    other = swap_core(other)

    n16, do, rkeep, rsend = call(
        outs_kernel, [wide, all1, four, four], 0, mine, other, reads, dn, us=1.6
    )

    rrecv = swap_core(rsend)
    parts = call(
        pair_back_kernel, [one] * 4 + [two] * 4, 0, rkeep, rrecv, early_t, n16,
        scratch=hold + hold2,
    )
    chunks = around_dp(parts[4:])
    own = parts[0]
    parts = around_z(parts[:4])

    def early_grads(half, token, *done):
        return call(
            functools.partial(early_grads_kernel, half),
            [((C, 4 * (1 + half) * C), bf16)] + [four] * 4 + [one, ((H, C), f32)],
            0, mine, other, uw, do, inside, attn, kn, qn, growth, iq, *done, us=2.2, after=(token,),
        )

    early0 = early_grads(0, own)
    early1 = early_grads(1, own, early0[0])
    mixed = lax.dot_general(n16, out_weight, NN, preferred_element_type=f32).astype(bf16)
    reach, total = call(group_back_kernel, [four, one], 0, *parts, maps)
    parts = around_x([total] * 4)
    wkeep, wsend = call(
        wgrad_kernel,
        [((16, 8, 2048), f32)] * 2,
        0, *chunks, cot, below, above, lower, upper, us=2.5, after=(total, early1[1]),
    )
    wrecv = swap_core(wsend)
    wparts = call(wsum_pair_kernel, [((4, 8, 2048), f32)] * 4, 0, wkeep, wrecv)
    parts = call(
        enter_back_kernel, [one] * 4, 0, *parts, totals, maps, reach, us=1.5, scratch=hold + hold,
        after=(wparts[0], mixed),
    )
    parts = around_z(parts)
    wsent = around_x(wparts)
    wparts = call(wsum_first_kernel, [((8, 2048), f32)] * 4, 0, *wsent)
    dmine, dother = call(
        split_pair_back_kernel, [four] * 2, 0, *parts, late_t, rkeep, rrecv, scratch=hold,
        after=(wparts[0],),
    )
    dother = swap_core(dother)
    dk, dv, db, dg, mark = call(
        late_grads_kernel,
        [wide, wide, ((H, C), f32), ((H, C), f32), ((H, C), f32)],
        0, v, mine, other, dmine, dother, inside, kk, kn, invt, growth, fading, beta, ik, last_decay,
        *early0[1:], *early1[1:], us=6, after=(wparts[0],),
    )
    wparts = around_z(wparts)
    scale = 1.0 / math.sqrt(n_all)

    def last(a0, a1, a2, a3, out):
        wsum_last_kernel(scale, a0, a1, a2, a3, out)

    (weight_grad,) = call(last, [((8, 2048), f32)], 0, *wparts, after=(mark,))
    dq = early1[0]
    return (mixed[None], dq[None], dk[None], dv[None], db.T[None], dg.T[None], weight_grad)


def solution(mesh):
    rows = P("dp", "seq", None)
    return jax.shard_map(
        local,
        mesh=mesh,
        in_specs=(rows, rows, rows, rows, rows, P("dp", "seq"), P(), rows),
        out_specs=(rows, rows, rows, rows, rows, rows, P(("dp", "seq"), None)),
        check_vma=False,
    )
```

```python
import functools
import math

import jax
import jax.numpy as jnp
from jax import lax
from jax.experimental import pallas as pl
from jax.experimental.pallas import tpu as pltpu
from jax.sharding import PartitionSpec as P

f32 = jnp.float32
bf16 = jnp.bfloat16
EPS = 1e-06
C = 128
H = 8
VMEM_LIMIT = 24 * 1024 * 1024
FIRST_LIMIT = 62 * 1024 * 1024

NN = (((1,), (0,)), ((), ()))
NT = (((1,), (1,)), ((), ()))
TN = (((0,), (0,)), ((), ()))


def split(x):
    hi = x.astype(bf16)
    return hi, (x - hi.astype(f32)).astype(bf16)


def dot(a, b, dims=NN):
    return lax.dot_general(a, b, dims, preferred_element_type=f32)


def mm(a, b, dims=NN):
    ah, al = split(a)
    bh, bl = split(b)
    left = jnp.concatenate([ah, al], axis=1)
    n = dims[0][1][0]
    if b.shape[1 - n] > C:
        return dot(left, jnp.concatenate([bh, bh], axis=n), dims) + dot(ah, bl, dims)
    right = jnp.concatenate([bh, bl], axis=1 - n)
    both = dot(left, jnp.concatenate([right, right], axis=n), dims)
    return both[:, :C] + both[:, C:]


def tn(a, b):
    return mm(a.T, b)


def split3(x):
    hi = x.astype(bf16)
    rest = x - hi.astype(f32)
    mid = rest.astype(bf16)
    return hi, mid, (rest - mid.astype(f32)).astype(bf16)


def iotas(shape=(C, C)):
    return lax.broadcasted_iota(jnp.int32, shape, 0), lax.broadcasted_iota(jnp.int32, shape, 1)


def head(ref, h):
    return ref[:, h * C : (h + 1) * C].astype(f32)


def unit(x):
    inv = 1.0 / jnp.sqrt(jnp.sum(x * x, axis=-1, keepdims=True) + EPS)
    return x * inv, inv


def gate_tables(resets, b_ref, g_ref):
    rows, cols = iotas()
    lower = (rows >= cols).astype(bf16)
    upper = (rows <= cols).astype(bf16)
    parts = split3(g_ref[...])
    total_c = sum(dot(lower, part, NT) for part in parts)
    total_r = sum(dot(part, upper) for part in parts)
    beta = dot((rows == cols).astype(bf16), b_ref[...], NT)
    keep1 = 1.0 - resets[0, 0].astype(f32)
    keep2 = 1.0 - resets[0, 1].astype(f32)
    late = lax.broadcasted_iota(jnp.int32, (C, H), 0) >= 64
    growth = jnp.exp(total_c) * (keep1 * jnp.where(late, keep2, 1.0))
    last = total_c[C - 1 : C]
    fading = jnp.exp(last - total_c) * jnp.where(late, 1.0, keep2)
    g_last = jnp.exp(last) * (keep1 * keep2)
    doc = jnp.where((rows >= 64) & (cols < 64), keep2, 1.0)
    return total_c, total_r, growth, fading, g_last, beta, doc


def head_gates(tables, h):
    total_c, total_r, growth, fading, g_last, beta, doc = tables
    rows, cols = iotas()
    keep = rows >= cols
    later = total_c[:, h : h + 1] - total_r[h : h + 1, :]
    inside = jnp.where(keep, jnp.exp(jnp.where(keep, later, 0.0)), 0.0) * doc
    return inside, growth[:, h : h + 1], fading[:, h : h + 1], g_last[:, h : h + 1], beta[:, h : h + 1]


def place():
    seq = lax.axis_index("seq")
    return lax.axis_index("dp"), seq // 8, (seq // 2) % 4, seq % 2


def strict(x):
    rows, cols = iotas()
    return jnp.where(rows > cols, x, 0.0)


def spec_v(n):
    return [pl.BlockSpec(memory_space=pltpu.VMEM)] * n


def call(kernel, outs, n_smem, *args, us=1.0, scratch=(), hbm=(), after=(), limit=VMEM_LIMIT):
    n_after = len(after)

    def body(*refs):
        kernel(*refs[n_after:])

    in_specs = [pl.BlockSpec(memory_space=pl.ANY)] * n_after + [
        pl.BlockSpec(
            memory_space=pltpu.SMEM if i < n_smem else pltpu.HBM if i in hbm else pltpu.VMEM
        )
        for i in range(len(args))
    ]
    return pl.pallas_call(
        body,
        out_shape=[jax.ShapeDtypeStruct(s, d) for s, d in outs],
        in_specs=in_specs,
        out_specs=spec_v(len(outs)),
        scratch_shapes=list(scratch),
        compiler_params=pltpu.CompilerParams(vmem_limit_bytes=limit),
        cost_estimate=pl.CostEstimate(flops=0, bytes_accessed=1, transcendentals=0),
    )(*after, *args)


HEADS = range(H)


def maps_kernel(
    resets, b_ref, g_ref, k_hbm, v_hbm, cot_hbm, keep_ref, send_ref, inv_ref, uw_ref, wide_ref, k_ref, v_ref, cot_ref, sems
):
    load_k = pltpu.make_async_copy(k_hbm, k_ref, sems.at[0])
    load_v = pltpu.make_async_copy(v_hbm, v_ref, sems.at[1])
    load_cot = pltpu.make_async_copy(cot_hbm, cot_ref, sems.at[2])
    load_k.start()
    load_v.start()
    load_cot.start()
    tables = gate_tables(resets, b_ref, g_ref)
    rows, cols = iotas()
    eye = (rows == cols).astype(f32)
    block = (rows >= 64) == (cols >= 64)
    gates = [head_gates(tables, h) for h in HEADS]
    load_k.wait()
    kn = [unit(head(k_ref, h))[0] for h in HEADS]
    kk = [mm(kn[h], kn[h], NT) for h in HEADS]
    system = [strict(kk[h] * gates[h][0]) * gates[h][4] for h in HEADS]
    near = [jnp.where(block, x, 0.0) for x in system]
    far = [jnp.where(block, 0.0, x) for x in system]
    inv = [eye - x for x in near]
    power = [mm(x, x) for x in near]
    for level in range(5):
        if level < 4:
            both = [mm(jnp.concatenate([inv[h], power[h]], axis=0), power[h]) for h in HEADS]
            inv = [inv[h] + both[h][:C] for h in HEADS]
            power = [both[h][C:] for h in HEADS]
        else:
            inv = [inv[h] + mm(inv[h], power[h]) for h in HEADS]
    cross = [mm(far[h], inv[h]) for h in HEADS]
    inv = [inv[h] - mm(inv[h], cross[h]) for h in HEADS]
    load_cot.wait()
    wide_ref[...] = cot_ref[...].astype(f32)
    load_v.wait()
    uw = []
    for h in HEADS:
        bh = gates[h][4]
        right = jnp.concatenate([kn[h] * (bh * gates[h][1]), head(v_ref, h) * bh], axis=1)
        uw.append(mm(inv[h], right))
    maps = []
    for h in HEADS:
        prod = tn(kn[h] * gates[h][2], uw[h])
        maps.append(
            jnp.concatenate([eye * gates[h][3] - prod[:, :C], prod[:, C:]], axis=1)
        )
    for h in HEADS:
        inv_ref[h] = inv[h]
        uw_ref[h] = uw[h]
    first = place()[3] == 0
    for j in range(4):
        keep_ref[j] = jnp.where(first, maps[j], maps[j + 4])
        send_ref[j] = jnp.where(first, maps[j + 4], maps[j])


def compose(later, earlier):
    moved = mm(later[:, :C], earlier)
    return jnp.concatenate([moved[:, :C], moved[:, C:] + later[:, C:]], axis=1)


def pair_kernel(keep_ref, recv_ref, o0, o1, o2, o3, scratch):
    first = place()[3] == 0
    for j in range(4):
        a, b = keep_ref[j], recv_ref[j]
        early = jnp.where(first, a, b)
        late = jnp.where(first, b, a)
        scratch[j] = compose(late, early)
    for r, out in enumerate((o0, o1, o2, o3)):
        out[...] = scratch[(place()[2] + r) % 4]


def group_kernel(x0, x1, x2, x3, maps_ref, prefix_ref, total_ref):
    for r, ref in enumerate((x0, x1, x2, x3)):
        maps_ref[(place()[2] + 4 - r) % 4] = ref[...]
    run = maps_ref[0]
    prefix_ref[0] = run
    for i in range(1, 4):
        run = compose(maps_ref[i], run)
        if i < 3:
            prefix_ref[i] = run
    total_ref[...] = run


def enter_kernel(t0, t1, t2, t3, prefix_ref, totals_ref, o0, o1, o2, o3, scratch):
    for r, ref in enumerate((t0, t1, t2, t3)):
        totals_ref[(place()[1] + 4 - r) % 4] = ref[...]
    x = place()[1]
    s1 = totals_ref[0, :, C:]
    s2 = mm(totals_ref[1, :, :C], s1) + totals_ref[1, :, C:]
    s3 = mm(totals_ref[2, :, :C], s2) + totals_ref[2, :, C:]
    state = jnp.where(x == 0, 0.0, jnp.where(x == 1, s1, jnp.where(x == 2, s2, s3)))
    scratch[0] = state
    for i in range(3):
        scratch[i + 1] = mm(prefix_ref[i, :, :C], state) + prefix_ref[i, :, C:]
    for r, out in enumerate((o0, o1, o2, o3)):
        out[...] = scratch[(place()[2] + r) % 4]


def split_pair_kernel(s0, s1, s2, s3, keep_ref, recv_ref, mine_ref, other_ref, scratch):
    for r, ref in enumerate((s0, s1, s2, s3)):
        scratch[(place()[2] + 4 - r) % 4] = ref[...]
    first = place()[3] == 0
    for j in range(4):
        early = jnp.where(first, keep_ref[j], recv_ref[j])
        start = scratch[j]
        middle = mm(early[:, :C], start) + early[:, C:]
        mine_ref[j] = jnp.where(first, start, middle)
        other_ref[j] = jnp.where(first, middle, start)


def reads_kernel(
    resets, b_ref, g_ref, q_ref, k_ref, uw_ref, inv_ref, mkeep_ref, mrecv_ref,
    read_ref, inside_ref, attn_ref, kk_ref, kn_ref, qn_ref, invt_ref,
    growth_ref, fading_ref, beta_ref, iq_ref, ik_ref, last_ref, early_ref, late_ref,
):
    tables = gate_tables(resets, b_ref, g_ref)
    growth_ref[...] = tables[2]
    fading_ref[...] = tables[3]
    last_ref[...] = tables[4]
    beta_ref[...] = tables[5]
    cols = lax.broadcasted_iota(jnp.int32, (C, H), 1)
    iq_all = jnp.zeros((C, H), f32)
    ik_all = jnp.zeros((C, H), f32)
    for group in (range(0, 4), range(4, 8)):
        qn, kn, inside, attn = {}, {}, {}, {}
        for h in group:
            qn[h], iq = unit(head(q_ref, h))
            kn[h], ik = unit(head(k_ref, h))
            inside[h], growth, _, _, _ = head_gates(tables, h)
            iq_all = jnp.where(cols == h, iq, iq_all)
            ik_all = jnp.where(cols == h, ik, ik_all)
            inside_ref[h] = inside[h]
            kn_ref[h] = kn[h]
            qn_ref[h] = qn[h]
            invt_ref[h] = inv_ref[h].T
        inner = {h: mm(jnp.concatenate([qn[h], kn[h]], axis=0), kn[h], NT) for h in group}
        for h in group:
            attn[h] = inner[h][:C] * inside[h]
            attn_ref[h] = attn[h]
            kk_ref[h] = inner[h][C:]
        prod = {h: mm(attn[h], uw_ref[h]) for h in group}
        for h in group:
            growth = tables[2][:, h : h + 1]
            read_ref[h] = jnp.concatenate(
                [qn[h] * growth - prod[h][:, :C], prod[h][:, C:]], axis=1
            )
    first = place()[3] == 0
    for j in range(4):
        a, b = mkeep_ref[j, :, :C], mrecv_ref[j, :, :C]
        early_ref[j] = jnp.where(first, a, b).T
        late_ref[j] = jnp.where(first, b, a).T
    iq_ref[...] = iq_all
    ik_ref[...] = ik_all


def pick(first, mine_ref, other_ref, h):
    a, b = mine_ref[h % 4], other_ref[h % 4]
    return jnp.where(first, a, b) if h < 4 else jnp.where(first, b, a)


def outs_kernel(
    mine_ref, other_ref, read_ref, dn_ref, n_ref, do_ref, keep_ref, send_ref
):
    first = place()[3] == 0
    outs = [
        mm(read_ref[h, :, :C], pick(first, mine_ref, other_ref, h)) + read_ref[h, :, C:] for h in HEADS
    ]
    for h in HEADS:
        out = outs[h]
        inv = 1.0 / jnp.sqrt(jnp.mean(out * out, axis=-1, keepdims=True) + EPS)
        n32 = out * inv
        n_ref[:, h * C : (h + 1) * C] = n32.astype(bf16)
        dn = dn_ref[:, h * C : (h + 1) * C]
        do_ref[h] = inv * (dn - n32 * jnp.mean(n32 * dn, axis=-1, keepdims=True))
    reach = [tn(read_ref[h, :, :C], do_ref[h]) for h in HEADS]
    for j in range(4):
        keep_ref[j] = jnp.where(first, reach[j], reach[j + 4])
        send_ref[j] = jnp.where(first, reach[j + 4], reach[j])


def pair_back_kernel(
    keep_ref, recv_ref, early_ref, n_ref, o0, o1, o2, o3, c0, c1, c2, c3, scratch, wide
):
    for j in range(4):
        wide[j] = n_ref[:, 2 * j * C : 2 * (j + 1) * C].astype(f32)
    for r, out_ref in enumerate((c0, c1, c2, c3)):
        out_ref[...] = wide[(place()[0] + r) % 4]
    first = place()[3] == 0
    for j in range(4):
        a, b = keep_ref[j], recv_ref[j]
        early = jnp.where(first, a, b)
        late = jnp.where(first, b, a)
        scratch[j] = early + mm(early_ref[j], late)
    for r, out in enumerate((o0, o1, o2, o3)):
        out[...] = scratch[(place()[2] + r) % 4]


def group_back_kernel(r0, r1, r2, r3, maps_ref, reach_ref, total_ref):
    for r, ref in enumerate((r0, r1, r2, r3)):
        reach_ref[(place()[2] + 4 - r) % 4] = ref[...]
    run = reach_ref[3]
    for i in (2, 1, 0):
        run = reach_ref[i] + tn(maps_ref[i, :, :C], run)
    total_ref[...] = run


def enter_back_kernel(t0, t1, t2, t3, totals_ref, maps_ref, reach_ref, o0, o1, o2, o3, parts, scratch):
    for r, ref in enumerate((t0, t1, t2, t3)):
        parts[(place()[1] + 4 - r) % 4] = ref[...]
    x = place()[1]
    d2 = parts[3]
    d1 = parts[2] + tn(totals_ref[2, :, :C], d2)
    d0 = parts[1] + tn(totals_ref[1, :, :C], d1)
    run = jnp.where(x == 3, 0.0, jnp.where(x == 2, d2, jnp.where(x == 1, d1, d0)))
    scratch[3] = run
    for i in (2, 1, 0):
        run = reach_ref[i + 1] + tn(maps_ref[i + 1, :, :C], run)
        scratch[i] = run
    for r, out in enumerate((o0, o1, o2, o3)):
        out[...] = scratch[(place()[2] + r) % 4]


def split_pair_back_kernel(
    s0, s1, s2, s3, late_ref, keep_ref, recv_ref, mine_ref, other_ref, scratch
):
    for r, ref in enumerate((s0, s1, s2, s3)):
        scratch[(place()[2] + 4 - r) % 4] = ref[...]
    first = place()[3] == 0
    for j in range(4):
        late = jnp.where(first, recv_ref[j], keep_ref[j])
        end = scratch[j]
        middle = late + mm(late_ref[j], end)
        mine_ref[j] = jnp.where(first, middle, end)
        other_ref[j] = jnp.where(first, end, middle)


def early_grads_kernel(
    mine_ref, other_ref, uw_ref, do_ref, inside_ref, attn_ref, kn_ref, qn_ref, growth_ref, iq_ref,
    dq_ref, delta_ref, dkn_ref, dd_ref, carried_ref, rowpart_ref, colpart_ref,
):
    first = place()[3] == 0
    _, cols = iotas()
    row8 = lax.broadcasted_iota(jnp.int32, (H, C), 0)
    row_all = jnp.zeros((C, C), f32)
    col_all = jnp.zeros((H, C), f32)
    group = HEADS
    state = {h: pick(first, mine_ref, other_ref, h) for h in group}
    moved = {
        h: mm(jnp.concatenate([uw_ref[h, :, :C], kn_ref[h]], axis=0), state[h]) for h in group
    }
    delta = {h: uw_ref[h, :, C:] - moved[h][:C] for h in group}
    for h in group:
        dd_ref[h] = tn(attn_ref[h], do_ref[h])
        delta_ref[h] = delta[h]
        carried_ref[h] = moved[h][C:]
    both = {
        h: mm(do_ref[h], jnp.concatenate([delta[h], state[h]], axis=0), NT) for h in group
    }
    dqk = {h: both[h][:, :C] * inside_ref[h] for h in group}
    back = {h: both[h][:, C:] * growth_ref[:, h : h + 1] for h in group}
    dqn = {h: back[h] + mm(dqk[h], kn_ref[h]) for h in group}
    for h in group:
        dkn_ref[h] = tn(dqk[h], qn_ref[h])
    for h in group:
        qn = qn_ref[h]
        dq = iq_ref[:, h : h + 1] * (
            dqn[h] - qn * jnp.sum(dqn[h] * qn, axis=-1, keepdims=True)
        )
        dq_ref[:, h * C : (h + 1) * C] = dq.astype(bf16)
        pairs = both[h][:, :C] * attn_ref[h]
        row = jnp.sum(pairs + back[h] * qn, axis=-1, keepdims=True)
        row_all = jnp.where(cols == h, row, row_all)
        col_all = jnp.where(row8 == h, jnp.sum(pairs, axis=0, keepdims=True), col_all)
    rowpart_ref[...] = row_all
    colpart_ref[...] = col_all


EARLY = 6


def late_grads_kernel(
    v_ref, mine_ref, other_ref, dmine_ref, dother_ref, inside_ref, kk_ref, kn_ref, invt_ref,
    growth_ref, fading_ref, beta_ref, ik_ref, last_ref, *refs
):
    early = refs[:EARLY]
    dk_ref, dv_ref, db_ref, dg_ref, mark_ref = refs[EARLY:]
    first = place()[3] == 0
    rows, cols = iotas()
    row8 = lax.broadcasted_iota(jnp.int32, (H, C), 0)
    row_all = early[4][...]
    col_all = early[5][...]
    db_all = jnp.zeros((C, C), f32)
    is_last = lax.broadcasted_iota(jnp.int32, (C, 1), 0) == C - 1
    for group in (HEADS,):
        delta, dkn, dd, carried = (
            {h: early[part][h] for h in group} for part in range(4)
        )
        state = {h: pick(first, mine_ref, other_ref, h) for h in group}
        dstate = {h: pick(first, dmine_ref, dother_ref, h) for h in group}
        growth, fading, g_last, bh = (
            {h: ref[:, h : h + 1] for h in group} for ref in (growth_ref, fading_ref, last_ref, beta_ref)
        )
        ddelta = {h: dd[h] + mm(kn_ref[h], dstate[h]) * fading[h] for h in group}
        dkf = {h: mm(delta[h], dstate[h], NT) * fading[h] for h in group}
        dtarget = {h: mm(invt_ref[h], ddelta[h]) for h in group}
        both = {
            h: mm(dtarget[h], jnp.concatenate([delta[h], state[h]], axis=0), NT) for h in group
        }
        dsys = {h: -(both[h][:, :C] * strict(inside_ref[h])) for h in group}
        dkk = {h: dsys[h] * bh[h] for h in group}
        inner = {h: mm(dkk[h] + dkk[h].T, kn_ref[h]) for h in group}
        for h in group:
            dv_ref[:, h * C : (h + 1) * C] = (dtarget[h] * bh[h]).astype(bf16)
            raw = dsys[h] * kk_ref[h]
            dcar = dtarget[h] * carried[h] * growth[h]
            db = jnp.sum(dtarget[h] * head(v_ref, h) - dcar + raw, axis=-1, keepdims=True)
            pairs = raw * bh[h]
            dfade = dkf[h] * kn_ref[h]
            dlast = jnp.sum(dfade + g_last[h] * (state[h] * dstate[h]), axis=0, keepdims=True)
            dtotal = jnp.sum(pairs - dcar * bh[h] - dfade, axis=-1, keepdims=True)
            dtotal = dtotal + jnp.where(is_last, jnp.sum(dlast, axis=-1, keepdims=True), 0.0)
            grad = dkn[h] + inner[h] + dkf[h] - both[h][:, C:] * (bh[h] * growth[h])
            dk = ik_ref[:, h : h + 1] * (
                grad - kn_ref[h] * jnp.sum(grad * kn_ref[h], axis=-1, keepdims=True)
            )
            dk_ref[:, h * C : (h + 1) * C] = dk.astype(bf16)
            db_all = jnp.where(cols == h, db, db_all)
            row_all = row_all + jnp.where(cols == h, dtotal, 0.0)
            col_all = col_all + jnp.where(row8 == h, jnp.sum(pairs, axis=0, keepdims=True), 0.0)
    lower = (rows >= cols).astype(bf16)
    mark_ref[...] = col_all
    db_ref[...] = db_all.T[:H]
    dg_ref[...] = sum(dot(part, lower) for part in split3(row_all.T[:H] - col_all))


def relay_kernel(below_ref, above_ref, lower_ref, upper_ref):
    lower_ref[...] = below_ref[:64, :]
    upper_ref[...] = above_ref[64:, :]


def wgrad_kernel(n0, n1, n2, n3, c0, c1, c3, c2_low, c2_up, keep_ref, send_ref):
    ns = [ref[...].astype(bf16).T for ref in (n0, n1, n2, n3)]
    first = place()[3] == 0
    for j in range(8):
        cols = slice(j * 256, (j + 1) * 256)
        far = jnp.concatenate([c2_low[:, cols], c2_up[:, cols]], axis=0)
        cots = (c0[:, cols], c1[:, cols], far, c3[:, cols])
        total = sum(dot(ns[r], cots[r].astype(bf16)) for r in range(4)).reshape(16, 2, 8, 256)
        a, b = total[:, 0], total[:, 1]
        keep_ref[:, :, cols] = jnp.where(first, a, b)
        send_ref[:, :, cols] = jnp.where(first, b, a)


def wsum_pair_kernel(keep_ref, recv_ref, o0, o1, o2, o3):
    for r, out in enumerate((o0, o1, o2, o3)):
        x = (place()[1] + r) % 4
        for z in range(4):
            out[z] = keep_ref[4 * x + z] + recv_ref[4 * x + z]


def wsum_first_kernel(a0, a1, a2, a3, o0, o1, o2, o3):
    for r, out in enumerate((o0, o1, o2, o3)):
        z = (place()[2] + r) % 4
        out[...] = (a0[z] + a1[z]) + (a2[z] + a3[z])


def wsum_last_kernel(scale, a0, a1, a2, a3, out):
    out[...] = ((a0[...] + a1[...]) + (a2[...] + a3[...])) * scale


def seq_perm(dx, dz, dc=0):
    pairs = []
    for i in range(32):
        x, z, c = i // 8, (i // 2) % 4, i % 2
        pairs.append((i, ((x + dx) % 4) * 8 + ((z + dz) % 4) * 2 + (c ^ dc)))
    return pairs


def swap_core(x):
    return lax.ppermute(x, "seq", seq_perm(0, 0, 1))


def around_z(parts):
    moved = {r: lax.ppermute(parts[r], "seq", seq_perm(0, r)) for r in (1, 2, 3)}
    return [parts[0], moved[1], moved[2], moved[3]]


def around_x(parts):
    moved = {r: lax.ppermute(parts[r], "seq", seq_perm(r, 0)) for r in (1, 2, 3)}
    return [parts[0], moved[1], moved[2], moved[3]]


def step_dp(x, r):
    return lax.ppermute(x, "dp", [(i, (i + r) % 4) for i in range(4)])


def around_dp(parts):
    moved = {r: step_dp(parts[r], r) for r in (2, 1, 3)}
    return [parts[0], moved[1], moved[2], moved[3]]


def local(queries, keys, values, strength, log_decay, resets, out_weight, cotangent):
    q, k, v = queries[0], keys[0], values[0]
    cot = cotangent[0]
    gates = (resets, strength[0].T, log_decay[0].T)
    n_all = C * lax.axis_size("seq") * lax.axis_size("dp")

    mat, mat2 = (C, C), (C, 2 * C)
    one, two = (mat, f32), (mat2, f32)
    four, four2 = ((4, *mat), f32), ((4, *mat2), f32)
    all1, all2 = ((H, *mat), f32), ((H, *mat2), f32)
    wide = ((C, H * C), bf16)
    hold, hold2 = [pltpu.VMEM(*four)], [pltpu.VMEM(*four2)]

    mkeep, msend, inverse, uw, cot32 = call(
        maps_kernel,
        [four2, four2, all1, all2, ((C, 2048), f32)],
        1, *gates, k, v, cot, us=6, hbm=(3, 4, 5), limit=FIRST_LIMIT,
        scratch=[
            pltpu.VMEM(*wide), pltpu.VMEM(*wide), pltpu.VMEM((C, 2048), bf16), pltpu.SemaphoreType.DMA((3,)),
        ],
    )
    mrecv = swap_core(msend)
    parts = call(pair_kernel, [two] * 4, 0, mkeep, mrecv, scratch=hold2)
    own = parts[0]
    parts = around_z(parts)
    dn = lax.dot_general(cot, out_weight, NT, preferred_element_type=f32)
    below, above = step_dp(cot32, 1), step_dp(cot32, 3)
    maps, prefix, total = call(
        group_kernel, [four2, ((3, *mat2), f32), two], 0, *parts, after=(dn, cot32)
    )
    parts = around_x([total] * 4)
    reads, inside, attn, kk, kn, qn, invt, growth, fading, beta, iq, ik, last_decay, early_t, late_t = call(
        reads_kernel,
        [all2] + [all1] * 6 + [((C, H), f32)] * 5 + [((1, H), f32), four, four],
        1, *gates, q, k, uw, inverse, mkeep, mrecv, us=3, after=(total,),
    )
    totals, *parts = call(
        enter_kernel, [four2] + [one] * 4, 0, *parts, prefix, us=1.2, scratch=hold, after=(reads,)
    )
    own = parts[0]
    parts = around_z(parts)
    lower, upper = call(relay_kernel, [((64, 2048), f32)] * 2, 0, below, above, after=(own,))
    lower, upper = step_dp(lower, 1), step_dp(upper, 3)
    mine, other = call(split_pair_kernel, [four] * 2, 0, *parts, mkeep, mrecv, scratch=hold)
    other = swap_core(other)

    n16, do, rkeep, rsend = call(
        outs_kernel, [wide, all1, four, four], 0, mine, other, reads, dn, us=1.6
    )

    rrecv = swap_core(rsend)
    parts = call(
        pair_back_kernel, [one] * 4 + [two] * 4, 0, rkeep, rrecv, early_t, n16,
        scratch=hold + hold2,
    )
    chunks = around_dp(parts[4:])
    own = parts[0]
    parts = around_z(parts[:4])

    early = call(
        early_grads_kernel,
        [wide] + [all1] * 4 + [one, ((H, C), f32)],
        0, mine, other, uw, do, inside, attn, kn, qn, growth, iq, us=2.2, after=(own,),
    )
    mixed = lax.dot_general(n16, out_weight, NN, preferred_element_type=f32).astype(bf16)
    reach, total = call(group_back_kernel, [four, one], 0, *parts, maps)
    parts = around_x([total] * 4)
    wkeep, wsend = call(
        wgrad_kernel,
        [((16, 8, 2048), f32)] * 2,
        0, *chunks, cot, below, above, lower, upper, us=2.5, after=(total, early[1]),
    )
    wrecv = swap_core(wsend)
    wparts = call(wsum_pair_kernel, [((4, 8, 2048), f32)] * 4, 0, wkeep, wrecv)
    parts = call(
        enter_back_kernel, [one] * 4, 0, *parts, totals, maps, reach, us=1.5, scratch=hold + hold,
        after=(wparts[0], mixed),
    )
    parts = around_z(parts)
    wsent = around_x(wparts)
    wparts = call(wsum_first_kernel, [((8, 2048), f32)] * 4, 0, *wsent)
    dmine, dother = call(
        split_pair_back_kernel, [four] * 2, 0, *parts, late_t, rkeep, rrecv, scratch=hold,
        after=(wparts[0],),
    )
    dother = swap_core(dother)
    dk, dv, db, dg, mark = call(
        late_grads_kernel,
        [wide, wide, ((H, C), f32), ((H, C), f32), ((H, C), f32)],
        0, v, mine, other, dmine, dother, inside, kk, kn, invt, growth, fading, beta, ik, last_decay,
        *early[1:], us=6, after=(wparts[0],),
    )
    wparts = around_z(wparts)
    scale = 1.0 / math.sqrt(n_all)

    def last(a0, a1, a2, a3, out):
        wsum_last_kernel(scale, a0, a1, a2, a3, out)

    (weight_grad,) = call(last, [((8, 2048), f32)], 0, *wparts, after=(mark,))
    dq = early[0]
    return (mixed[None], dq[None], dk[None], dv[None], db.T[None], dg.T[None], weight_grad)


def solution(mesh):
    rows = P("dp", "seq", None)
    return jax.shard_map(
        local,
        mesh=mesh,
        in_specs=(rows, rows, rows, rows, rows, P("dp", "seq"), P(), rows),
        out_specs=(rows, rows, rows, rows, rows, rows, P(("dp", "seq"), None)),
        check_vma=False,
    )
```
